256 devices in a mesh: row: 16 (over z, y_hi), col: 16 (over y_lo, x, core).
Axes of the slice: x: 4, y: 4 (y_hi: 2, y_lo: 2; y = y_hi * 2 + y_lo), z: 8, core: 2. Of those that a mesh axis runs over, the one named last changes fastest.
Arguments:
- queries: bfloat16 [65536, 768], P(('row', 'col')), may hold values from -20 to 20
- keys: bfloat16 [65536, 768], P(('row', 'col')), may hold values from -20 to 20
- values: bfloat16 [65536, 768], P(('row', 'col')), may hold values from -6 to 6
- grad_out: bfloat16 [65536, 768], P(('row', 'col')), may hold values from -96 to 96
Outputs:
- grad_queries: bfloat16 [65536, 768], P(('row', 'col'))
- grad_keys: bfloat16 [65536, 768], P(('row', 'col'))
- grad_values: bfloat16 [65536, 768], P(('row', 'col'))
The draws below stay inside these ranges and needn't reach their ends.
All inputs are finite; a program needn't handle non-finite values.
Results may differ from the reference program's by a relative error of at most 0.0097.
Values may be sent and summed in bfloat16 or wider, within the bound.
A program may use at most 128 MiB of HBM per device.

```python
import jax
import jax.numpy as jnp
from jax import lax

HEADS = 12
HEAD_DIM = 64
TOK_DEV = 256
WIDTH = 768
TOKENS = 65536
N_ROW = 16
N_COL = 16


def draw_queries(key, part):
    key = jax.random.fold_in(key, 1)
    drawn = jnp.clip(jax.random.normal(key, (TOKENS, HEADS * HEAD_DIM), jnp.float32), -4.0, 4.0)
    return drawn.astype(jnp.bfloat16)


def draw_keys(key, part):
    key = jax.random.fold_in(key, 2)
    drawn = jnp.clip(jax.random.normal(key, (TOKENS, HEADS * HEAD_DIM), jnp.float32), -4.0, 4.0)
    return drawn.astype(jnp.bfloat16)


def shard_levels(stream_key, shape, cuts, least, high):
    gain = 1.0
    for axis_at, shards_of in cuts:
        draws = jax.random.uniform(jax.random.fold_in(jax.random.fold_in(stream_key, 6), axis_at), (shards_of,), jnp.float32, least / len(cuts), high / len(cuts))
        gain = gain * jnp.repeat(jnp.exp(draws), shape[axis_at] // shards_of).reshape((-1,) + (1,) * (len(shape) - 1 - axis_at))
    return gain


def normal_values(key, extent, width, limit, shards=(), kind=jnp.bfloat16):
    result = width * jax.random.normal(key, extent, jnp.float32)
    if shards:
        result = result * shard_levels(key, extent, shards, -0.22, 0.18)
    return jnp.clip(result, -limit, limit).astype(kind)


def setup_inputs(seed: int = 0) -> dict:
    seeds = jax.random.split(jax.random.key(seed), 5)
    queries = draw_queries(jax.random.fold_in(seeds[4], 71), 0)
    keys = draw_keys(jax.random.fold_in(seeds[4], 71), 0)
    values = normal_values(seeds[2], (TOKENS, WIDTH), 1.0, 6.0, ((0, 256),))
    grad_out = normal_values(seeds[3], (TOKENS, WIDTH), 16.0, 96.0, ((0, 256),))
    return dict(queries=queries, keys=keys, values=values, grad_out=grad_out)


NEG_FILL = -1.0e30


def onehot_table(stride):
    return jnp.arange(stride)[:, None] == (jnp.arange(HEADS) % stride)[None, :]


def pick_rows(whole_rows, stride):
    tail_dims = whole_rows.shape[2:]
    shaped = whole_rows.reshape((whole_rows.shape[0] // stride, stride, HEADS) + tail_dims)
    picker = onehot_table(stride).reshape((1, stride, HEADS) + (1,) * len(tail_dims))
    return jnp.sum(jnp.where(picker, shaped, jnp.zeros((), whole_rows.dtype)), axis=1).astype(whole_rows.dtype)


def place_rows(piece_rows, stride, fill_value):
    tail_dims = piece_rows.shape[2:]
    picker = onehot_table(stride).reshape((1, stride, HEADS) + (1,) * len(tail_dims))
    spread = jnp.where(picker, piece_rows[:, None], fill_value)
    return spread.reshape((piece_rows.shape[0] * stride, HEADS) + tail_dims)


def reference(queries, keys, values, grad_out):
    stride_list = (1, 4, N_COL, 4 * N_COL, N_ROW * N_COL)
    scale = HEAD_DIM ** -0.5
    query_heads = queries.reshape(TOKENS, HEADS, HEAD_DIM)
    key_heads = keys.reshape(TOKENS, HEADS, HEAD_DIM)
    value_heads = values.reshape(TOKENS, HEADS, HEAD_DIM)
    grad_heads = grad_out.reshape(TOKENS, HEADS, HEAD_DIM)
    segs_shape = (-1, TOK_DEV, HEADS, HEAD_DIM)

    def kept(array, stride):
        return pick_rows(array, stride).reshape(segs_shape)

    def forward_segment(items):
        seg_q, seg_k, seg_v = items
        scores = jnp.einsum("qhd,khd->hqk", seg_q.astype(jnp.float32), seg_k.astype(jnp.float32)) * scale
        row_max = jnp.max(scores, axis=2)
        weights = jnp.exp(scores - row_max[:, :, None])
        row_sum = jnp.sum(weights, axis=2)
        weights_low = weights.astype(jnp.bfloat16).astype(jnp.float32)
        partial_value = jnp.einsum("hqk,khd->qhd", weights_low, seg_v.astype(jnp.float32))
        return row_max.T, row_sum.T, partial_value

    maxima, sums, partials = [], [], []
    for stride in stride_list:
        row_max, row_sum, partial_value = lax.map(forward_segment, (kept(query_heads, stride), kept(key_heads, stride), kept(value_heads, stride)))
        maxima.append(place_rows(row_max.reshape(-1, HEADS), stride, NEG_FILL))
        sums.append(place_rows(row_sum.reshape(-1, HEADS), stride, 0.0))
        partials.append(place_rows(partial_value.reshape(-1, HEADS, HEAD_DIM), stride, 0.0))
    total_max = maxima[0]
    for item in maxima[1:]:
        total_max = jnp.maximum(total_max, item)
    norm = jnp.zeros((TOKENS, HEADS), jnp.float32)
    output = jnp.zeros((TOKENS, HEADS, HEAD_DIM), jnp.float32)
    for index in range(len(stride_list)):
        factor = jnp.exp(maxima[index] - total_max)
        norm = norm + sums[index] * factor
        output = output + partials[index] * factor[:, :, None]
    output = output / norm[:, :, None]
    lse = total_max + jnp.log(norm)
    delta = jnp.sum(grad_heads.astype(jnp.float32) * output, axis=2)

    def backward_segment(items):
        seg_q, seg_k, seg_v, seg_g, seg_lse, seg_delta = items
        fq, fk, fv, fg = (seg_q.astype(jnp.float32), seg_k.astype(jnp.float32), seg_v.astype(jnp.float32), seg_g.astype(jnp.float32))
        scores = jnp.einsum("qhd,khd->hqk", fq, fk) * scale
        probs = jnp.exp(scores - seg_lse.T[:, :, None])
        probs_low = probs.astype(jnp.bfloat16).astype(jnp.float32)
        dprob = jnp.einsum("qhd,khd->hqk", fg, fv)
        dscore = (probs * (dprob - seg_delta.T[:, :, None])).astype(jnp.bfloat16).astype(jnp.float32)
        grad_q = jnp.einsum("hqk,khd->qhd", dscore, fk) * scale
        grad_k = jnp.einsum("hqk,qhd->khd", dscore, fq) * scale
        grad_v = jnp.einsum("hqk,qhd->khd", probs_low, fg)
        return grad_q, grad_k, grad_v

    grad_q_all = jnp.zeros((TOKENS, HEADS, HEAD_DIM), jnp.float32)
    grad_k_all = jnp.zeros((TOKENS, HEADS, HEAD_DIM), jnp.float32)
    grad_v_all = jnp.zeros((TOKENS, HEADS, HEAD_DIM), jnp.float32)
    for stride in stride_list:
        seg_lse = pick_rows(lse, stride).reshape(-1, TOK_DEV, HEADS)
        seg_delta = pick_rows(delta, stride).reshape(-1, TOK_DEV, HEADS)
        grad_q, grad_k, grad_v = lax.map(backward_segment, (kept(query_heads, stride), kept(key_heads, stride), kept(value_heads, stride), kept(grad_heads, stride), seg_lse, seg_delta))
        grad_q_all = grad_q_all + place_rows(grad_q.reshape(-1, HEADS, HEAD_DIM), stride, 0.0)
        grad_k_all = grad_k_all + place_rows(grad_k.reshape(-1, HEADS, HEAD_DIM), stride, 0.0)
        grad_v_all = grad_v_all + place_rows(grad_v.reshape(-1, HEADS, HEAD_DIM), stride, 0.0)
    return (grad_q_all.reshape(TOKENS, WIDTH).astype(jnp.bfloat16), grad_k_all.reshape(TOKENS, WIDTH).astype(jnp.bfloat16), grad_v_all.reshape(TOKENS, WIDTH).astype(jnp.bfloat16))
```

```python
import jax
import jax.numpy as jnp
from jax import lax
from jax.experimental import pallas as pl
from jax.experimental.pallas import tpu as pltpu
from jax.sharding import PartitionSpec as P

HEADS = 12
HEAD_DIM = 64
TOK = 256
WIDTH = 768
LANES = 128
SCALE = HEAD_DIM**-0.5
NEG_FILL = -1e30
PAIRS = HEADS // 2
MESH = pl.DeviceIdType.MESH
F32 = jnp.float32
BF16 = jnp.bfloat16


def mm(a, b):
    return lax.dot_general(a, b, (((1,), (0,)), ((), ())), preferred_element_type=F32)


def mm_nt(a, b):
    return lax.dot_general(a, b, (((1,), (1,)), ((), ())), preferred_element_type=F32)


def mm_tn(a, b):
    return lax.dot_general(a, b, (((0,), (0,)), ((), ())), preferred_element_type=F32)


def iota(shape, dim):
    return lax.broadcasted_iota(jnp.int32, shape, dim)


def onehot(hit, value=1.0):
    return jnp.where(hit, value, 0.0).astype(BF16)


def move(rows, table):
    high = rows.astype(BF16)
    rest = rows - high.astype(F32)
    middle = rest.astype(BF16)
    low = (rest - middle.astype(F32)).astype(BF16)
    return mm(high, table) + mm(middle, table) + mm(low, table)


def swap(tile):
    return pltpu.roll(tile, HEAD_DIM, 1)


def reversed_digits(index):
    return (index & 3) * 64 + ((index >> 2) & 3) * 16 + ((index >> 4) & 3) * 4 + (index >> 6)


def forward(scores, dprob):
    row_max = jnp.max(scores, axis=0, keepdims=True)
    weights = jnp.exp(scores - row_max)
    row_sum = jnp.sum(weights, axis=0, keepdims=True)
    dot_sum = jnp.sum(weights * dprob, axis=0, keepdims=True)
    return weights, stat_tile(row_max + jnp.log(row_sum), dot_sum / row_sum, row_max)


def stat_tile(lse, delta, row_max):
    row = iota((8, TOK), 0)
    return jnp.where(row == 0, lse, jnp.where(row == 1, delta, jnp.where(row == 2, row_max, 0.0)))


def backward(weights, dprob, row_max, lse, delta):
    probs = weights * jnp.exp(row_max - lse)
    dscore = probs * (dprob - delta)
    return probs.astype(BF16), dscore.astype(BF16)


def merge(parts):
    top = parts[0][0]
    for lse, _ in parts[1:]:
        top = jnp.maximum(top, lse)
    norm = 0.0
    total = 0.0
    for lse, delta in parts:
        factor = jnp.exp(lse - top)
        norm = norm + factor
        total = total + factor * delta
    return top + jnp.log(norm), total / norm


def rows_of(tile):
    return tile[0:1], tile[1:2]


def masked_rows(tile, hit):
    lse, delta = rows_of(tile)
    return jnp.where(hit, lse, NEG_FILL), jnp.where(hit, delta, 0.0)


def kernel(
    q_ref, k_ref, v_ref, g_ref, dq_ref, dk_ref, dv_ref,
    qp, kp, vp, gp, acc_q, acc_k, acc_v,
    w_all, d_all, pack, recv_a, recv_l, sel_c, sel_d,
    st1, st2, st_l, fin1, fin2, fin_l, st3,
    a_own, b_own, c_two, d_two, e_four, f_five, g_three, h_three, i_three, j_three,
    out2, out_l, back4, back5, back2, back3,
    send_sem, recv_sem,
):
    row = lax.axis_index("row")
    col = lax.axis_index("col")
    member = lax.rem(col, 4)
    group = col // 4
    row_in = lax.rem(row, 4)
    row_group = row // 4
    is3 = col < HEADS
    is4 = jnp.logical_and(col >= HEADS, row_in < 3)
    is5 = jnp.logical_and(jnp.logical_and(col >= HEADS, row_in == 3), row_group < 3)
    has_long = jnp.logical_or(is3, jnp.logical_or(is4, is5))
    is45 = jnp.logical_or(is4, is5)
    row4, col4 = row_group * 4 + group, HEADS + member
    row5 = group * 4 + 3
    head4 = row_in * 4 + (col - HEADS)
    head5 = row_group * 4 + (col - HEADS)
    col_of4 = jnp.where(is4, head4, 0)
    col_of5 = jnp.where(is5, head5, 0)

    sends = []

    def post(src, dst, recv, to_row, to_col, cond=None, maybe_self=False):
        slot = len(sends)
        copy = pltpu.make_async_remote_copy(
            src_ref=src, dst_ref=dst, send_sem=send_sem.at[slot], recv_sem=recv_sem.at[recv],
            device_id=(to_row, to_col), device_id_type=MESH,
        )
        away = cond
        if maybe_self:
            same = jnp.logical_and(to_col == col, to_row == row)
            other = jnp.logical_not(same)
            away = other if cond is None else jnp.logical_and(cond, other)
            here = same if cond is None else jnp.logical_and(cond, same)

            @pl.when(here)
            def _():
                pltpu.make_async_copy(src, dst, recv_sem.at[recv]).start()

        if away is None:
            copy.start()
        else:
            pl.when(away)(copy.start)
        sends.append((away, copy))

    def arrive(buffer, recv):
        pltpu.make_async_copy(buffer, buffer, recv_sem.at[recv]).wait()

    barrier = pltpu.get_barrier_semaphore()

    def greet(to_row, to_col):
        pl.semaphore_signal(barrier, inc=1, device_id=(to_row, to_col), device_id_type=MESH)

    for apart in range(1, 16):
        greet(row, lax.rem(col + apart, 16))

    @pl.when(is3)
    def _():
        greet(row4, col4)
        greet(row5, col4)

    @pl.when(is4)
    def _():
        for step in range(4):
            greet(row_group * 4 + step, col_of4)

    @pl.when(is5)
    def _():
        for step in range(16):
            greet(step, col_of5)

    order = reversed_digits(iota((TOK, TOK), 0)) == iota((TOK, TOK), 1)
    permute = onehot(order)
    permute_scaled = onehot(order, SCALE)
    qp[...] = mm(permute_scaled, q_ref[...]).astype(BF16)
    kp[...] = mm(permute, k_ref[...]).astype(BF16)
    vp[...] = mm(permute, v_ref[...]).astype(BF16)
    gp[...] = mm(permute, g_ref[...]).astype(BF16)

    low64 = iota((64, LANES), 1) < HEAD_DIM
    low256 = iota((TOK, LANES), 1) < HEAD_DIM

    for w in range(4):
        rows = slice(64 * w, 64 * w + 64)
        for i in range(3):
            tile = slice(LANES * (2 * i + w // 2), LANES * (2 * i + w // 2) + LANES)
            for slot, (first, second) in enumerate(((qp, gp), (kp, vp))):
                one = first[rows, tile].astype(F32)
                two = second[rows, tile].astype(F32)
                if w % 2 == 0:
                    two = swap(two)
                else:
                    one = swap(one)
                pack[w, i, slot] = jnp.where(low64, one, two).astype(BF16)

    pl.semaphore_wait(barrier, 15 + jnp.where(is3, 2, jnp.where(is4, 4, jnp.where(is5, 16, 0))))

    for h in range(HEADS):
        w, i = h % 4, h // 4
        post(
            pack.at[w, i, :, pl.ds(16 * i, 16), :],
            recv_l.at[:, pl.ds(pl.multiple_of(16 * col, 16), 16), :],
            1, row, h, maybe_self=True,
        )
    my_rows = pl.ds(pl.multiple_of(64 * member, 64), 64)
    for apart in (2, 3, 1):
        w = lax.rem(member + apart, 4)
        post(pack.at[w], recv_a.at[:, :, my_rows, :], 0, row, group * 4 + w)
    pltpu.make_async_copy(pack.at[member], recv_a.at[:, :, my_rows, :], recv_sem.at[0]).start()

    def pair_forward(j, carry):
        lanes = pl.ds(pl.multiple_of(j * LANES, LANES), LANES)
        q, k, v, g = qp[:, lanes], kp[:, lanes], vp[:, lanes], gp[:, lanes]
        zero = jnp.zeros_like(k)
        i = j // 2
        for parity in range(2):
            mine = low256 if parity == 0 else jnp.logical_not(low256)
            scores = mm_nt(jnp.where(mine, k, zero), q)
            dprob = mm_nt(jnp.where(mine, v, zero), g)
            weights, stat = forward(scores, dprob)
            w_all[2 * j + parity] = weights
            d_all[2 * j + parity] = dprob
            st1[2 * lax.rem(j, 2) + parity, i] = stat
        return carry

    def packed_forward(query_side, key_side, unit):
        zero = jnp.zeros_like(key_side)
        scores = mm_nt(jnp.where(low256, key_side, zero), query_side)
        dprob = mm_nt(jnp.where(low256, zero, key_side), query_side)
        weights, stat = forward(scores, dprob)
        w_all[unit] = weights
        d_all[unit] = dprob
        return stat

    lax.fori_loop(0, 3, pair_forward, 0)

    @pl.when(is3)
    def _():
        arrive(recv_l, 1)
        pick4 = onehot(
            iota((64, TOK), 1) == 16 * (iota((64, TOK), 0) >> 2) + (iota((64, TOK), 0) & 3)
        )
        pick5 = onehot(iota((16, TOK), 1) == 16 * iota((16, TOK), 0))
        for slot in range(2):
            sel_c[slot] = mm(pick4, recv_l[slot]).astype(BF16)
            sel_d[slot] = mm(pick5, recv_l[slot]).astype(BF16)

    post(sel_c, recv_l.at[:, pl.ds(pl.multiple_of(64 * row_in, 64), 64), :], 1, row4, col4, cond=is3)
    post(sel_d, recv_l.at[:, pl.ds(pl.multiple_of(16 * row, 16), 16), :], 1, row5, col4, cond=is3)

    lax.fori_loop(3, PAIRS, pair_forward, 0)

    for h in range(HEADS):
        w, i = h % 4, h // 4
        post(
            st1.at[w, i, :, pl.ds(LANES * (w // 2), LANES)], a_own.at[col], 2, row, h,
            maybe_self=True,
        )
    for apart in range(4):
        w = lax.rem(member + apart, 4)
        post(
            st1.at[w, :, :, pl.ds(pl.multiple_of(LANES * (w // 2), LANES), LANES)],
            b_own.at[member], 3, row, group * 4 + w, maybe_self=True,
        )

    arrive(recv_a, 0)
    for i in range(3):
        st2[i] = packed_forward(recv_a[i, 0], recv_a[i, 1], HEADS + i)
    for i in range(3):
        post(st2.at[i], d_two.at[group], 5, row, member + 4 * i, maybe_self=True)
    for apart in range(4):
        w = lax.rem(member + apart, 4)
        post(
            st2.at[:, :, pl.ds(pl.multiple_of(LANES * (w // 2), LANES), LANES)],
            c_two.at[member], 4, row, group * 4 + w, maybe_self=True,
        )

    @pl.when(is45)
    def _():
        arrive(recv_l, 1)

    @pl.when(has_long)
    def _():
        st_l[...] = packed_forward(recv_l[0], recv_l[1], HEADS + 3)

    for step in range(4):
        post(
            st_l.at[:, pl.ds(LANES * (step // 2), LANES)], e_four, 6,
            row_group * 4 + step, col_of4, cond=is4,
        )
    for step in range(16):
        post(
            st_l.at[:, pl.ds(LANES * (step // 8), LANES)], f_five, 7, step, col_of5, cond=is5
        )

    lane = iota((1, TOK), 1)
    src128 = iota((LANES, TOK), 0)
    dst128 = iota((LANES, TOK), 1)
    src256 = iota((TOK, TOK), 0)
    dst256 = iota((TOK, TOK), 1)

    def picked(moved, count, hit):
        total = jnp.zeros((8, TOK), F32)
        for step in range(count):
            total = total + jnp.where(hit(step), moved[step], 0.0)
        return total

    @pl.when(is3)
    def _():
        arrive(a_own, 2)
        start = 64 * lax.rem(member, 2) + 16 * group
        one = move(
            a_own[...].reshape(16 * 8, LANES), onehot(src128 == start + (dst128 & 15))
        ).reshape(16, 8, TOK)
        one = rows_of(picked(one, 16, lambda c: (lane >> 4) == c))
        arrive(d_two, 5)
        two = move(
            d_two[...].reshape(4 * 8, TOK),
            onehot(src256 == 64 * ((dst256 >> 4) & 3) + 16 * group + (dst256 & 15)),
        ).reshape(4, 8, TOK)
        two = rows_of(picked(two, 4, lambda c: (lane >> 6) == c))
        arrive(e_four, 6)
        four = move(
            e_four[...],
            onehot(
                jnp.logical_and(
                    src128 == 64 * lax.rem(row_in, 2) + 4 * (dst128 >> 4) + (dst128 & 15),
                    (dst128 & 15) < 4,
                )
            ),
        )
        four = masked_rows(four, (lane & 15) < 4)
        arrive(f_five, 7)
        five = move(
            f_five[...],
            onehot(
                jnp.logical_and(
                    src128 == 16 * lax.rem(row, 8) + (dst128 >> 4), (dst128 & 15) == 0
                )
            ),
        )
        five = masked_rows(five, (lane & 15) == 0)
        lse, delta = merge([one, two, rows_of(st_l[...]), four, five])
        st3[...] = stat_tile(lse, delta, 0.0)
        fin_l[...] = stat_tile(lse, delta, 0.0)

    post(st3, i_three.at[row_in], 10, row4, col4, cond=is3)
    post(st3, j_three.at[row], 11, row5, col4, cond=is3)
    col_head = jnp.where(is3, col, 0)
    for step in range(4):
        post(
            st3.at[:, pl.ds(LANES * (step // 2), LANES)], h_three.at[jnp.where(is3, group, 0)], 9,
            row, step * 4 + member, cond=is3, maybe_self=True,
        )
    for step in range(16):
        post(
            st3.at[:, pl.ds(LANES * (step // 8), LANES)], g_three.at[col_head], 8,
            row, step, cond=is3, maybe_self=True,
        )

    @pl.when(is4)
    def _():
        arrive(i_three, 10)
        total = move(
            i_three[...].reshape(4 * 8, TOK),
            onehot(src256 == 16 * ((dst256 >> 2) & 15) + (dst256 & 3)),
        ).reshape(4, 8, TOK)
        fin_l[...] = picked(total, 4, lambda c: (lane >> 6) == c)

    @pl.when(is5)
    def _():
        arrive(j_three, 11)
        total = move(
            j_three[...].reshape(16 * 8, TOK), onehot(src256 == 16 * (dst256 & 15))
        ).reshape(16, 8, TOK)
        fin_l[...] = picked(total, 16, lambda c: (lane >> 4) == c)

    def packed_backward(query_side, key_side, unit, stat, final):
        probs, dscore = backward(
            w_all[unit], d_all[unit], stat[2:3], final[0:1], final[1:2]
        )
        zero = jnp.zeros_like(key_side)
        both = mm(dscore, jnp.where(low256, query_side, zero)) + mm(
            probs, jnp.where(low256, zero, query_side)
        )
        return both, mm_tn(dscore, jnp.where(low256, key_side, zero))

    @pl.when(has_long)
    def _():
        both, own = packed_backward(recv_l[0], recv_l[1], HEADS + 3, st_l[...], fin_l[...])
        out_l[0] = both.astype(BF16)
        out_l[1] = own.astype(BF16)

    for step in range(4):
        post(
            out_l.at[:, pl.ds(64 * step, 64), :], back4, 12,
            row_group * 4 + step, col_of4, cond=is4,
        )
    for step in range(16):
        post(out_l.at[:, pl.ds(16 * step, 16), :], back5, 13, step, col_of5, cond=is5)

    spread64 = onehot(src128 == 64 * lax.rem(member, 2) + (dst128 & 63))
    arrive(b_own, 3)
    arrive(h_three, 9)
    own2 = move(b_own[...].reshape(4 * 3 * 8, LANES), spread64).reshape(4, 3, 8, TOK)
    long2 = move(
        h_three[...].reshape(3 * 8, LANES),
        onehot(src128 == 64 * lax.rem(group, 2) + 16 * (dst128 >> 6) + (dst128 & 15)),
    ).reshape(3, 8, TOK)
    for i in range(3):
        one = rows_of(picked(own2[:, i], 4, lambda c: (lane >> 6) == c))
        lse, delta = merge([one, rows_of(st2[i])])
        long = ((lane >> 4) & 3) == i
        fin2[i] = stat_tile(
            jnp.where(long, long2[i][0:1], lse), jnp.where(long, long2[i][1:2], delta), 0.0
        )

    def two_backward(i, carry):
        both, own = packed_backward(recv_a[i, 0], recv_a[i, 1], HEADS + i, st2[i], fin2[i])
        out2[i, 0] = both.astype(BF16)
        out2[i, 1] = own.astype(BF16)
        return carry

    lax.fori_loop(0, 3, two_backward, 0)
    for apart in range(4):
        w = lax.rem(member + apart, 4)
        post(
            out2.at[:, :, pl.ds(pl.multiple_of(64 * w, 64), 64), :],
            back2.at[member], 14, row, group * 4 + w, maybe_self=True,
        )

    @pl.when(is3)
    def _():
        place4 = onehot(
            iota((TOK, 64), 0) == 16 * (iota((TOK, 64), 1) >> 2) + (iota((TOK, 64), 1) & 3)
        )
        place5 = onehot(iota((TOK, 16), 0) == 16 * iota((TOK, 16), 1))
        arrive(back4, 12)
        arrive(back5, 13)
        for slot in range(2):
            total = out_l[slot].astype(F32) + mm(place4, back4[slot]) + mm(place5, back5[slot])
            out_l[slot] = total.astype(BF16)

    for step in range(16):
        post(
            out_l.at[:, pl.ds(16 * step, 16), :], back3.at[col_head], 15,
            row, step, cond=is3, maybe_self=True,
        )

    arrive(c_two, 4)
    arrive(g_three, 8)
    two1 = move(c_two[...].reshape(HEADS * 8, LANES), spread64).reshape(4, 3, 8, TOK)
    three1 = move(
        g_three[...].reshape(HEADS * 8, LANES),
        onehot(src128 == 16 * lax.rem(col, 8) + (dst128 & 15)),
    ).reshape(HEADS, 8, TOK)
    for h in range(HEADS):
        w, i = h % 4, h // 4
        one = rows_of(st1[w, i])
        lse, delta = merge([one, masked_rows(two1[w, i], (lane >> 6) == w)])
        long = (lane >> 4) == 4 * w + i
        fin1[h] = stat_tile(
            jnp.where(long, three1[h][0:1], lse), jnp.where(long, three1[h][1:2], delta), 0.0
        )

    def pair_backward(j, carry):
        lanes = pl.ds(pl.multiple_of(j * LANES, LANES), LANES)
        q, k, g = qp[:, lanes], kp[:, lanes], gp[:, lanes]
        zero = jnp.zeros_like(k)
        i = j // 2
        sum_q = sum_k = sum_v = 0.0
        for parity in range(2):
            mine = low256 if parity == 0 else jnp.logical_not(low256)
            h = 2 * j + parity
            stat = st1[2 * lax.rem(j, 2) + parity, i]
            final = fin1[h]
            probs, dscore = backward(w_all[h], d_all[h], stat[2:3], final[0:1], final[1:2])
            sum_v = sum_v + mm(probs, jnp.where(mine, g, zero))
            sum_k = sum_k + mm(dscore, jnp.where(mine, q, zero))
            sum_q = sum_q + mm_tn(dscore, jnp.where(mine, k, zero))
        acc_q[:, lanes] = sum_q
        acc_k[:, lanes] = sum_k
        acc_v[:, lanes] = sum_v
        return carry

    lax.fori_loop(0, PAIRS, pair_backward, 0)

    arrive(back2, 14)
    arrive(back3, 15)
    for h in range(HEADS):
        w, i = h % 4, h // 4
        tile = slice(LANES * (2 * i + w // 2), LANES * (2 * i + w // 2) + LANES)
        for count, start, both, own in (
            (64, 64 * w, back2[w, i, 0], back2[w, i, 1]),
            (16, 64 * w + 16 * i, back3[h, 0], back3[h, 1]),
        ):
            rows = slice(start, start + count)
            low = iota((count, LANES), 1) < HEAD_DIM
            both = both.astype(F32)
            own = own.astype(F32)
            other = swap(both)
            if w % 2 == 0:
                grad_k = jnp.where(low, both, 0.0)
                grad_v = jnp.where(low, other, 0.0)
            else:
                grad_k = jnp.where(low, 0.0, other)
                grad_v = jnp.where(low, 0.0, both)
                own = swap(own)
            acc_q[rows, tile] += own
            acc_k[rows, tile] += grad_k
            acc_v[rows, tile] += grad_v
    dq_ref[...] = mm(permute_scaled, acc_q[...].astype(BF16)).astype(BF16)
    dk_ref[...] = mm(permute, acc_k[...].astype(BF16)).astype(BF16)
    dv_ref[...] = mm(permute, acc_v[...].astype(BF16)).astype(BF16)

    for away, copy in sends:
        if away is None:
            copy.wait_send()
        else:
            pl.when(away)(copy.wait_send)


def body(queries, keys, values, grad_out):
    def vm(shape, kind):
        return pltpu.VMEM(shape, kind)

    whole = pl.BlockSpec(memory_space=pltpu.VMEM)
    return pl.pallas_call(
        kernel,
        out_shape=[jax.ShapeDtypeStruct((TOK, WIDTH), BF16)] * 3,
        in_specs=[whole] * 4,
        out_specs=[whole] * 3,
        scratch_shapes=[vm((TOK, WIDTH), BF16)] * 4
        + [vm((TOK, WIDTH), F32)] * 3
        + [
            vm((16, TOK, TOK), F32),
            vm((16, TOK, TOK), F32),
            vm((4, 3, 2, 64, LANES), BF16),
            vm((3, 2, TOK, LANES), BF16),
            vm((2, TOK, LANES), BF16),
            vm((2, 64, LANES), BF16),
            vm((2, 16, LANES), BF16),
            vm((4, 3, 8, TOK), F32),
            vm((3, 8, TOK), F32),
            vm((8, TOK), F32),
            vm((HEADS, 8, TOK), F32),
            vm((3, 8, TOK), F32),
            vm((8, TOK), F32),
            vm((8, TOK), F32),
            vm((16, 8, LANES), F32),
            vm((4, 3, 8, LANES), F32),
            vm((4, 3, 8, LANES), F32),
            vm((4, 8, TOK), F32),
            vm((8, LANES), F32),
            vm((8, LANES), F32),
            vm((HEADS, 8, LANES), F32),
            vm((3, 8, LANES), F32),
            vm((4, 8, TOK), F32),
            vm((16, 8, TOK), F32),
            vm((3, 2, TOK, LANES), BF16),
            vm((2, TOK, LANES), BF16),
            vm((2, 64, LANES), BF16),
            vm((2, 16, LANES), BF16),
            vm((4, 3, 2, 64, LANES), BF16),
            vm((HEADS, 2, 16, LANES), BF16),
            pltpu.SemaphoreType.DMA((128,)),
            pltpu.SemaphoreType.DMA((16,)),
        ],
        compiler_params=pltpu.CompilerParams(
            collective_id=0, has_side_effects=True, vmem_limit_bytes=48 * 1024 * 1024
        ),
    )(queries, keys, values, grad_out)


def solution(mesh):
    spec = P(("row", "col"), None)
    return jax.shard_map(
        body, mesh=mesh, in_specs=(spec,) * 4, out_specs=(spec,) * 3, check_vma=False
    )
```

```python
import jax
import jax.numpy as jnp
from jax import lax
from jax.experimental import pallas as pl
from jax.experimental.pallas import tpu as pltpu
from jax.sharding import PartitionSpec as P

HEADS = 12
HEAD_DIM = 64
TOK = 256
WIDTH = 768
LANES = 128
SCALE = HEAD_DIM**-0.5
NEG_FILL = -1e30
PAIRS = HEADS // 2
MESH = pl.DeviceIdType.MESH
F32 = jnp.float32
BF16 = jnp.bfloat16


def mm(a, b):
    return lax.dot_general(a, b, (((1,), (0,)), ((), ())), preferred_element_type=F32)


def mm_nt(a, b):
    return lax.dot_general(a, b, (((1,), (1,)), ((), ())), preferred_element_type=F32)


def mm_tn(a, b):
    return lax.dot_general(a, b, (((0,), (0,)), ((), ())), preferred_element_type=F32)


def iota(shape, dim):
    return lax.broadcasted_iota(jnp.int32, shape, dim)


def onehot(hit, value=1.0):
    return jnp.where(hit, value, 0.0).astype(BF16)


def move(rows, table):
    high = rows.astype(BF16)
    rest = rows - high.astype(F32)
    middle = rest.astype(BF16)
    low = (rest - middle.astype(F32)).astype(BF16)
    return mm(high, table) + mm(middle, table) + mm(low, table)


def swap(tile):
    return pltpu.roll(tile, HEAD_DIM, 1)


def reversed_digits(index):
    return (index & 3) * 64 + ((index >> 2) & 3) * 16 + ((index >> 4) & 3) * 4 + (index >> 6)


def forward(scores, dprob):
    row_max = jnp.max(scores, axis=0, keepdims=True)
    weights = jnp.exp(scores - row_max)
    row_sum = jnp.sum(weights, axis=0, keepdims=True)
    dot_sum = jnp.sum(weights * dprob, axis=0, keepdims=True)
    return weights, stat_tile(row_max + jnp.log(row_sum), dot_sum / row_sum, row_max)


def stat_tile(lse, delta, row_max):
    row = iota((8, TOK), 0)
    return jnp.where(row == 0, lse, jnp.where(row == 1, delta, jnp.where(row == 2, row_max, 0.0)))


def backward(weights, dprob, row_max, lse, delta):
    probs = weights * jnp.exp(row_max - lse)
    dscore = probs * (dprob - delta)
    return probs.astype(BF16), dscore.astype(BF16)


def merge(parts):
    top = parts[0][0]
    for lse, _ in parts[1:]:
        top = jnp.maximum(top, lse)
    norm = 0.0
    total = 0.0
    for lse, delta in parts:
        factor = jnp.exp(lse - top)
        norm = norm + factor
        total = total + factor * delta
    return top + jnp.log(norm), total / norm


def rows_of(tile):
    return tile[0:1], tile[1:2]


def masked_rows(tile, hit):
    lse, delta = rows_of(tile)
    return jnp.where(hit, lse, NEG_FILL), jnp.where(hit, delta, 0.0)


def kernel(
    q_hbm, k_hbm, v_hbm, g_hbm, sum_q, sum_k, sum_v,
    q_in, k_in, v_in, g_in, qp, kp, vp, gp, acc_q, acc_k, acc_v,
    w_all, d_all, pack, recv_a, recv3, recv4, recv5, sel4, sel5,
    st1, st2, st_l, fin1, fin2, st3,
    a_own, b_own, c_two, d_two, g_three, h_three, i_three, j_three,
    out2, out_l, part4, part5, back2, back3,
    send_sem, recv_sem, load_sem,
):
    row = lax.axis_index("row")
    col = lax.axis_index("col")
    member = lax.rem(col, 4)
    group = col // 4
    row_in = lax.rem(row, 4)
    row_group = row // 4
    is3 = col < HEADS

    loads = []
    for slot, (src, dst) in enumerate(
        ((q_hbm, q_in), (g_hbm, g_in), (k_hbm, k_in), (v_hbm, v_in))
    ):
        load = pltpu.make_async_copy(src, dst, load_sem.at[slot])
        load.start()
        loads.append(load)

    sends = []

    def post(src, dst, recv, to_row, to_col, cond=None, maybe_self=False):
        slot = len(sends)
        copy = pltpu.make_async_remote_copy(
            src_ref=src, dst_ref=dst, send_sem=send_sem.at[slot], recv_sem=recv_sem.at[recv],
            device_id=(to_row, to_col), device_id_type=MESH,
        )
        away = cond
        if maybe_self:
            same = jnp.logical_and(to_col == col, to_row == row)
            other = jnp.logical_not(same)
            away = other if cond is None else jnp.logical_and(cond, other)
            here = same if cond is None else jnp.logical_and(cond, same)

            @pl.when(here)
            def _():
                pltpu.make_async_copy(src, dst, recv_sem.at[recv]).start()

        if away is None:
            copy.start()
        else:
            pl.when(away)(copy.start)
        sends.append((away, copy))

    def arrive(buffer, recv):
        pltpu.make_async_copy(buffer, buffer, recv_sem.at[recv]).wait()

    barrier = pltpu.get_barrier_semaphore()

    def greet(to_row, to_col):
        pl.semaphore_signal(barrier, inc=1, device_id=(to_row, to_col), device_id_type=MESH)

    for apart in range(1, 16):
        greet(row, lax.rem(col + apart, 16))

    @pl.when(is3)
    def _():
        for apart in range(1, 16):
            greet(lax.rem(row + apart, 16), col)

    order = reversed_digits(iota((TOK, TOK), 0)) == iota((TOK, TOK), 1)
    permute = onehot(order)
    permute_scaled = onehot(order, SCALE)
    for load, table, src, dst in zip(
        loads,
        (permute_scaled, permute, permute, permute),
        (q_in, g_in, k_in, v_in),
        (qp, gp, kp, vp),
    ):
        load.wait()
        dst[...] = mm(table, src[...]).astype(BF16)

    low64 = iota((64, LANES), 1) < HEAD_DIM
    low256 = iota((TOK, LANES), 1) < HEAD_DIM

    for w in range(4):
        rows = slice(64 * w, 64 * w + 64)
        for i in range(3):
            tile = slice(LANES * (2 * i + w // 2), LANES * (2 * i + w // 2) + LANES)
            for slot, (first, second) in enumerate(((qp, gp), (kp, vp))):
                one = first[rows, tile].astype(F32)
                two = second[rows, tile].astype(F32)
                if w % 2 == 0:
                    two = swap(two)
                else:
                    one = swap(one)
                pack[w, i, slot] = jnp.where(low64, one, two).astype(BF16)

    pl.semaphore_wait(barrier, jnp.where(is3, 30, 15))

    for h in range(HEADS):
        w, i = h % 4, h // 4
        post(
            pack.at[w, i, :, pl.ds(16 * i, 16), :],
            recv3.at[:, pl.ds(pl.multiple_of(16 * col, 16), 16), :],
            1, row, h, maybe_self=True,
        )
    my_rows = pl.ds(pl.multiple_of(64 * member, 64), 64)
    for apart in (2, 3, 1):
        w = lax.rem(member + apart, 4)
        post(pack.at[w], recv_a.at[:, :, my_rows, :], 0, row, group * 4 + w)
    pltpu.make_async_copy(pack.at[member], recv_a.at[:, :, my_rows, :], recv_sem.at[0]).start()

    def pair_forward(j, carry):
        lanes = pl.ds(pl.multiple_of(j * LANES, LANES), LANES)
        q, k, v, g = qp[:, lanes], kp[:, lanes], vp[:, lanes], gp[:, lanes]
        zero = jnp.zeros_like(k)
        i = j // 2
        for parity in range(2):
            mine = low256 if parity == 0 else jnp.logical_not(low256)
            scores = mm_nt(jnp.where(mine, k, zero), q)
            dprob = mm_nt(jnp.where(mine, v, zero), g)
            weights, stat = forward(scores, dprob)
            w_all[2 * j + parity] = weights
            d_all[2 * j + parity] = dprob
            st1[2 * lax.rem(j, 2) + parity, i] = stat
        return carry

    def packed_forward(query_side, key_side, unit):
        zero = jnp.zeros_like(key_side)
        scores = mm_nt(jnp.where(low256, key_side, zero), query_side)
        dprob = mm_nt(jnp.where(low256, zero, key_side), query_side)
        weights, stat = forward(scores, dprob)
        w_all[unit] = weights
        d_all[unit] = dprob
        return stat

    lax.fori_loop(0, PAIRS, pair_forward, 0)

    @pl.when(is3)
    def _():
        arrive(recv3, 1)
        pick4 = onehot(
            iota((64, TOK), 1) == 16 * (iota((64, TOK), 0) >> 2) + (iota((64, TOK), 0) & 3)
        )
        pick5 = onehot(iota((16, TOK), 1) == 16 * iota((16, TOK), 0))
        for slot in range(2):
            sel4[slot] = mm(pick4, recv3[slot]).astype(BF16)
            sel5[slot] = mm(pick5, recv3[slot]).astype(BF16)

    rows4 = pl.ds(pl.multiple_of(64 * row_in, 64), 64)
    rows5 = pl.ds(pl.multiple_of(16 * row, 16), 16)

    def across(src, dst, count, recv):
        for apart in range(1, count):
            to_row = lax.rem(row + apart, 16) if count == 16 else (
                row_group * 4 + lax.rem(row_in + apart, 4)
            )
            post(src, dst, recv, to_row, col, cond=is3)

        @pl.when(is3)
        def _():
            pltpu.make_async_copy(src, dst, recv_sem.at[recv]).start()

    across(sel5, recv5.at[:, rows5, :], 16, 7)
    across(sel4, recv4.at[:, rows4, :], 4, 6)

    for h in range(HEADS):
        w, i = h % 4, h // 4
        post(
            st1.at[w, i, :, pl.ds(LANES * (w // 2), LANES)], a_own.at[col], 2, row, h,
            maybe_self=True,
        )
    for apart in range(4):
        w = lax.rem(member + apart, 4)
        post(
            st1.at[w, :, :, pl.ds(pl.multiple_of(LANES * (w // 2), LANES), LANES)],
            b_own.at[member], 3, row, group * 4 + w, maybe_self=True,
        )

    arrive(recv_a, 0)
    for i in range(3):
        st2[i] = packed_forward(recv_a[i, 0], recv_a[i, 1], HEADS + i)
    for i in range(3):
        post(st2.at[i], d_two.at[group], 5, row, member + 4 * i, maybe_self=True)
    for apart in range(4):
        w = lax.rem(member + apart, 4)
        post(
            st2.at[:, :, pl.ds(pl.multiple_of(LANES * (w // 2), LANES), LANES)],
            c_two.at[member], 4, row, group * 4 + w, maybe_self=True,
        )


    @pl.when(is3)
    def _():
        st_l[0] = packed_forward(recv3[0], recv3[1], 15)
        arrive(recv4, 6)
        st_l[1] = packed_forward(recv4[0], recv4[1], 16)
        arrive(recv5, 7)
        st_l[2] = packed_forward(recv5[0], recv5[1], 17)

    lane = iota((1, TOK), 1)
    src128 = iota((LANES, TOK), 0)
    dst128 = iota((LANES, TOK), 1)
    src256 = iota((TOK, TOK), 0)
    dst256 = iota((TOK, TOK), 1)

    def picked(moved, count, hit):
        total = jnp.zeros((8, TOK), F32)
        for step in range(count):
            total = total + jnp.where(hit(step), moved[step], 0.0)
        return total

    @pl.when(is3)
    def _():
        arrive(a_own, 2)
        start = 64 * lax.rem(member, 2) + 16 * group
        one = move(
            a_own[...].reshape(16 * 8, LANES), onehot(src128 == start + (dst128 & 15))
        ).reshape(16, 8, TOK)
        one = rows_of(picked(one, 16, lambda c: (lane >> 4) == c))
        arrive(d_two, 5)
        two = move(
            d_two[...].reshape(4 * 8, TOK),
            onehot(src256 == 64 * ((dst256 >> 4) & 3) + 16 * group + (dst256 & 15)),
        ).reshape(4, 8, TOK)
        two = rows_of(picked(two, 4, lambda c: (lane >> 6) == c))
        four = move(
            st_l[1],
            onehot(
                jnp.logical_and(
                    src256 == 64 * row_in + 4 * (dst256 >> 4) + (dst256 & 15),
                    (dst256 & 15) < 4,
                )
            ),
        )
        four = masked_rows(four, (lane & 15) < 4)
        five = move(
            st_l[2],
            onehot(
                jnp.logical_and(src256 == 16 * row + (dst256 >> 4), (dst256 & 15) == 0)
            ),
        )
        five = masked_rows(five, (lane & 15) == 0)
        lse, delta = merge([one, two, rows_of(st_l[0]), four, five])
        st3[...] = stat_tile(lse, delta, 0.0)

    across(st3, j_three.at[row], 16, 11)
    across(st3, i_three.at[row_in], 4, 10)
    col_head = jnp.where(is3, col, 0)
    for step in range(4):
        post(
            st3.at[:, pl.ds(LANES * (step // 2), LANES)], h_three.at[jnp.where(is3, group, 0)], 9,
            row, step * 4 + member, cond=is3, maybe_self=True,
        )
    for step in range(16):
        post(
            st3.at[:, pl.ds(LANES * (step // 8), LANES)], g_three.at[col_head], 8,
            row, step, cond=is3, maybe_self=True,
        )

    def packed_backward(query_side, key_side, unit, stat, final):
        probs, dscore = backward(
            w_all[unit], d_all[unit], stat[2:3], final[0:1], final[1:2]
        )
        zero = jnp.zeros_like(key_side)
        both = mm(dscore, jnp.where(low256, query_side, zero)) + mm(
            probs, jnp.where(low256, zero, query_side)
        )
        return both, mm_tn(dscore, jnp.where(low256, key_side, zero))

    spread64 = onehot(src128 == 64 * lax.rem(member, 2) + (dst128 & 63))
    arrive(b_own, 3)
    arrive(h_three, 9)
    own2 = move(b_own[...].reshape(4 * 3 * 8, LANES), spread64).reshape(4, 3, 8, TOK)
    long2 = move(
        h_three[...].reshape(3 * 8, LANES),
        onehot(src128 == 64 * lax.rem(group, 2) + 16 * (dst128 >> 6) + (dst128 & 15)),
    ).reshape(3, 8, TOK)
    for i in range(3):
        one = rows_of(picked(own2[:, i], 4, lambda c: (lane >> 6) == c))
        lse, delta = merge([one, rows_of(st2[i])])
        long = ((lane >> 4) & 3) == i
        fin2[i] = stat_tile(
            jnp.where(long, long2[i][0:1], lse), jnp.where(long, long2[i][1:2], delta), 0.0
        )

    def two_backward(i, carry):
        both, own = packed_backward(recv_a[i, 0], recv_a[i, 1], HEADS + i, st2[i], fin2[i])
        out2[i, 0] = both.astype(BF16)
        out2[i, 1] = own.astype(BF16)
        return carry

    lax.fori_loop(0, 3, two_backward, 0)
    for apart in range(4):
        w = lax.rem(member + apart, 4)
        post(
            out2.at[:, :, pl.ds(pl.multiple_of(64 * w, 64), 64), :],
            back2.at[member], 14, row, group * 4 + w, maybe_self=True,
        )

    @pl.when(is3)
    def _():
        both3, own3 = packed_backward(recv3[0], recv3[1], 15, st_l[0], st3[...])
        arrive(i_three, 10)
        total = move(
            i_three[...].reshape(4 * 8, TOK),
            onehot(src256 == 16 * ((dst256 >> 2) & 15) + (dst256 & 3)),
        ).reshape(4, 8, TOK)
        total = picked(total, 4, lambda c: (lane >> 6) == c)
        both4, own4 = packed_backward(recv4[0], recv4[1], 16, st_l[1], total)
        part4[0] = both4
        part4[1] = own4
        arrive(j_three, 11)
        total = move(
            j_three[...].reshape(16 * 8, TOK), onehot(src256 == 16 * (dst256 & 15))
        ).reshape(16, 8, TOK)
        total = picked(total, 16, lambda c: (lane >> 4) == c)
        both5, own5 = packed_backward(recv5[0], recv5[1], 17, st_l[2], total)
        part5[0] = both5
        part5[1] = own5
        place4 = onehot(
            iota((TOK, 64), 0) == 16 * (iota((TOK, 64), 1) >> 2) + (iota((TOK, 64), 1) & 3)
        )
        place5 = onehot(iota((TOK, 16), 0) == 16 * iota((TOK, 16), 1))
        for slot, base in enumerate((both3, own3)):
            total = (
                base
                + mm(place4, part4[slot, rows4, :].astype(BF16))
                + mm(place5, part5[slot, rows5, :].astype(BF16))
            )
            out_l[slot] = total.astype(BF16)

    for step in range(16):
        post(
            out_l.at[:, pl.ds(16 * step, 16), :], back3.at[col_head], 15,
            row, step, cond=is3, maybe_self=True,
        )

    arrive(c_two, 4)
    arrive(g_three, 8)
    two1 = move(c_two[...].reshape(HEADS * 8, LANES), spread64).reshape(4, 3, 8, TOK)
    three1 = move(
        g_three[...].reshape(HEADS * 8, LANES),
        onehot(src128 == 16 * lax.rem(col, 8) + (dst128 & 15)),
    ).reshape(HEADS, 8, TOK)
    for h in range(HEADS):
        w, i = h % 4, h // 4
        one = rows_of(st1[w, i])
        lse, delta = merge([one, masked_rows(two1[w, i], (lane >> 6) == w)])
        long = (lane >> 4) == 4 * w + i
        fin1[h] = stat_tile(
            jnp.where(long, three1[h][0:1], lse), jnp.where(long, three1[h][1:2], delta), 0.0
        )

    def pair_backward(j, carry):
        lanes = pl.ds(pl.multiple_of(j * LANES, LANES), LANES)
        q, k, g = qp[:, lanes], kp[:, lanes], gp[:, lanes]
        zero = jnp.zeros_like(k)
        i = j // 2
        sum_q = sum_k = sum_v = 0.0
        for parity in range(2):
            mine = low256 if parity == 0 else jnp.logical_not(low256)
            h = 2 * j + parity
            stat = st1[2 * lax.rem(j, 2) + parity, i]
            final = fin1[h]
            probs, dscore = backward(w_all[h], d_all[h], stat[2:3], final[0:1], final[1:2])
            sum_v = sum_v + mm(probs, jnp.where(mine, g, zero))
            sum_k = sum_k + mm(dscore, jnp.where(mine, q, zero))
            sum_q = sum_q + mm_tn(dscore, jnp.where(mine, k, zero))
        acc_q[:, lanes] = sum_q
        acc_k[:, lanes] = sum_k
        acc_v[:, lanes] = sum_v
        return carry

    lax.fori_loop(0, PAIRS, pair_backward, 0)

    arrive(back2, 14)
    arrive(back3, 15)
    for h in range(HEADS):
        w, i = h % 4, h // 4
        tile = slice(LANES * (2 * i + w // 2), LANES * (2 * i + w // 2) + LANES)
        for count, start, both, own in (
            (64, 64 * w, back2[w, i, 0], back2[w, i, 1]),
            (16, 64 * w + 16 * i, back3[h, 0], back3[h, 1]),
        ):
            rows = slice(start, start + count)
            low = iota((count, LANES), 1) < HEAD_DIM
            both = both.astype(F32)
            own = own.astype(F32)
            other = swap(both)
            if w % 2 == 0:
                grad_k = jnp.where(low, both, 0.0)
                grad_v = jnp.where(low, other, 0.0)
            else:
                grad_k = jnp.where(low, 0.0, other)
                grad_v = jnp.where(low, 0.0, both)
                own = swap(own)
            acc_q[rows, tile] += own
            acc_k[rows, tile] += grad_k
            acc_v[rows, tile] += grad_v
    sum_q[...] = acc_q[...].astype(BF16)
    sum_k[...] = acc_k[...].astype(BF16)
    sum_v[...] = acc_v[...].astype(BF16)

    for away, copy in sends:
        if away is None:
            copy.wait_send()
        else:
            pl.when(away)(copy.wait_send)


def restore(sum_q, sum_k, sum_v, dq_hbm, dk_hbm, dv_hbm, dq, dk, dv, sems):
    order = reversed_digits(iota((TOK, TOK), 0)) == iota((TOK, TOK), 1)
    copies = []
    for slot, (src, tile, dst) in enumerate(
        ((sum_q, dq, dq_hbm), (sum_k, dk, dk_hbm), (sum_v, dv, dv_hbm))
    ):
        table = onehot(order, SCALE if slot == 0 else 1.0)
        tile[...] = mm(table, src[...]).astype(BF16)
        copy = pltpu.make_async_copy(tile, dst, sems.at[slot])
        copy.start()
        copies.append(copy)
    for copy in copies:
        copy.wait()


def body(queries, keys, values, grad_out):
    vm = pltpu.VMEM
    whole = pl.BlockSpec(memory_space=pltpu.VMEM)
    hbm = pl.BlockSpec(memory_space=pltpu.HBM)
    array = jax.ShapeDtypeStruct((TOK, WIDTH), BF16)
    queries, keys, values, grad_out = [
        pltpu.with_memory_space_constraint(x, pltpu.HBM) for x in (queries, keys, values, grad_out)
    ]
    sums = pl.pallas_call(
        kernel,
        out_shape=[array] * 3,
        in_specs=[hbm] * 4,
        out_specs=[whole] * 3,
        scratch_shapes=[vm((TOK, WIDTH), BF16)] * 8
        + [vm((TOK, WIDTH), F32)] * 3
        + [
            vm((18, TOK, TOK), F32),
            vm((18, TOK, TOK), F32),
            vm((4, 3, 2, 64, LANES), BF16),
            vm((3, 2, TOK, LANES), BF16),
            vm((2, TOK, LANES), BF16),
            vm((2, TOK, LANES), BF16),
            vm((2, TOK, LANES), BF16),
            vm((2, 64, LANES), BF16),
            vm((2, 16, LANES), BF16),
            vm((4, 3, 8, TOK), F32),
            vm((3, 8, TOK), F32),
            vm((3, 8, TOK), F32),
            vm((HEADS, 8, TOK), F32),
            vm((3, 8, TOK), F32),
            vm((8, TOK), F32),
            vm((16, 8, LANES), F32),
            vm((4, 3, 8, LANES), F32),
            vm((4, 3, 8, LANES), F32),
            vm((4, 8, TOK), F32),
            vm((HEADS, 8, LANES), F32),
            vm((3, 8, LANES), F32),
            vm((4, 8, TOK), F32),
            vm((16, 8, TOK), F32),
            vm((3, 2, TOK, LANES), BF16),
            vm((2, TOK, LANES), BF16),
            vm((2, TOK, LANES), F32),
            vm((2, TOK, LANES), F32),
            vm((4, 3, 2, 64, LANES), BF16),
            vm((HEADS, 2, 16, LANES), BF16),
            pltpu.SemaphoreType.DMA((128,)),
            pltpu.SemaphoreType.DMA((16,)),
            pltpu.SemaphoreType.DMA((4,)),
        ],
        compiler_params=pltpu.CompilerParams(
            collective_id=0, has_side_effects=True, vmem_limit_bytes=48 * 1024 * 1024
        ),
    )(queries, keys, values, grad_out)
    return pl.pallas_call(
        restore,
        out_shape=[array] * 3,
        in_specs=[whole] * 3,
        out_specs=[hbm] * 3,
        scratch_shapes=[vm((TOK, WIDTH), BF16)] * 3 + [pltpu.SemaphoreType.DMA((3,))],
        compiler_params=pltpu.CompilerParams(vmem_limit_bytes=16 * 1024 * 1024),
    )(*sums)


def solution(mesh):
    spec = P(("row", "col"), None)
    return jax.shard_map(
        body, mesh=mesh, in_specs=(spec,) * 4, out_specs=(spec,) * 3, check_vma=False
    )
```

```python
import jax
import jax.numpy as jnp
from jax import lax
from jax.experimental import pallas as pl
from jax.experimental.pallas import tpu as pltpu
from jax.sharding import PartitionSpec as P

HEADS = 12
HEAD_DIM = 64
TOK = 256
WIDTH = 768
LANES = 128
SCALE = HEAD_DIM**-0.5
NEG_FILL = -1e30
PAIRS = HEADS // 2
MESH = pl.DeviceIdType.MESH
FAR_FIRST = (8, 9, 7, 10, 6, 11, 5, 12, 4, 13, 3, 14, 2, 15, 1)
F32 = jnp.float32
BF16 = jnp.bfloat16


def mm(a, b):
    return lax.dot_general(a, b, (((1,), (0,)), ((), ())), preferred_element_type=F32)


def mm_nt(a, b):
    return lax.dot_general(a, b, (((1,), (1,)), ((), ())), preferred_element_type=F32)


def mm_tn(a, b):
    return lax.dot_general(a, b, (((0,), (0,)), ((), ())), preferred_element_type=F32)


def iota(shape, dim):
    return lax.broadcasted_iota(jnp.int32, shape, dim)


def onehot(hit, value=1.0):
    return jnp.where(hit, value, 0.0).astype(BF16)


def move(rows, table):
    count = rows.shape[0]
    high = rows.astype(BF16).astype(F32)
    rest = rows - high
    middle = rest.astype(BF16).astype(F32)
    parts = jnp.concatenate([high, middle, rest - middle], axis=0).astype(BF16)
    moved = mm(parts, table)
    return moved[:count] + moved[count : 2 * count] + moved[2 * count :]


def swap(tile):
    return pltpu.roll(tile, HEAD_DIM, 1)


def reversed_digits(index):
    return (index & 3) * 64 + ((index >> 2) & 3) * 16 + ((index >> 4) & 3) * 4 + (index >> 6)


def forward(scores, dprob):
    row_max = jnp.max(scores, axis=0, keepdims=True)
    weights = jnp.exp(scores - row_max)
    row_sum = jnp.sum(weights, axis=0, keepdims=True)
    dot_sum = jnp.sum(weights * dprob, axis=0, keepdims=True)
    return weights, stat_tile(row_max + jnp.log(row_sum), dot_sum / row_sum, row_max)


def stat_tile(lse, delta, row_max):
    row = iota((8, TOK), 0)
    return jnp.where(row == 0, lse, jnp.where(row == 1, delta, jnp.where(row == 2, row_max, 0.0)))


def backward(weights, dprob, row_max, lse, delta):
    probs = weights * jnp.exp(row_max - lse)
    dscore = probs * (dprob - delta)
    return probs.astype(BF16), dscore.astype(BF16)


def merge(parts):
    top = parts[0][0]
    for lse, _ in parts[1:]:
        top = jnp.maximum(top, lse)
    norm = 0.0
    total = 0.0
    for lse, delta in parts:
        factor = jnp.exp(lse - top)
        norm = norm + factor
        total = total + factor * delta
    return top + jnp.log(norm), total / norm


def rows_of(tile):
    return tile[0:1], tile[1:2]


def masked_rows(tile, hit):
    lse, delta = rows_of(tile)
    return jnp.where(hit, lse, NEG_FILL), jnp.where(hit, delta, 0.0)


def kernel(
    q_hbm, k_hbm, v_hbm, g_hbm, sum_q, sum_k, sum_v,
    q_in, k_in, v_in, g_in, qp, kp, vp, gp, acc_q, acc_k, acc_v,
    w_all, d_all, pack, recv_a, recv3, recv4, recv5, sel4, sel5,
    st1, st2, st_l, fin1, fin2, st3, st4_out, st5_out,
    a_own, b_own, c_two, d_two, g_three, h_three, i_three, j_three,
    tab_a, tab_d, tab_out, tab_64, tab_16, tab_h, tab_p4, tab_p5,
    out2, out_l, base3, keyed4, keyed5, back2, back3,
    send_sem, recv_sem, load_sem,
):
    row = lax.axis_index("row")
    col = lax.axis_index("col")
    member = lax.rem(col, 4)
    group = col // 4
    row_in = lax.rem(row, 4)
    row_group = row // 4
    is3 = col < HEADS

    loads = []
    for slot, (src, dst) in enumerate(
        ((q_hbm, q_in), (g_hbm, g_in), (k_hbm, k_in), (v_hbm, v_in))
    ):
        load = pltpu.make_async_copy(src, dst, load_sem.at[slot])
        load.start()
        loads.append(load)

    barrier = pltpu.get_barrier_semaphore()

    def greet(to_row, to_col):
        pl.semaphore_signal(barrier, inc=1, device_id=(to_row, to_col), device_id_type=MESH)

    @pl.when(is3)
    def _():
        for apart in FAR_FIRST:
            greet(lax.rem(row + apart, 16), col)

    for apart in range(1, 16):
        greet(row, lax.rem(col + apart, 16))

    slots = iter(range(144))
    sent_all, sent3, sent_not3 = [], [], []

    def remote(src, dst, recv, to_row, to_col, into, like=None):
        slot = next(slots)
        copy = pltpu.make_async_remote_copy(
            src_ref=src, dst_ref=dst, send_sem=send_sem.at[slot],
            recv_sem=recv_sem.at[recv], device_id=(to_row, to_col), device_id_type=MESH,
        )
        if like is None:
            into.append(copy.wait_send)
        else:
            into.append(lambda: pltpu.make_async_copy(like(), like(), send_sem.at[slot]).wait())
        return copy

    def local(src, dst, recv):
        pltpu.make_async_copy(src, dst, recv_sem.at[recv]).start()

    def arrive(buffer, recv):
        pltpu.make_async_copy(buffer, buffer, recv_sem.at[recv]).wait()

    def to_workers(source, dst, recv):
        base = jnp.where(is3, col, 3 * (col - HEADS))
        for apart in range(HEADS):
            h = lax.rem(base + apart, HEADS)
            src = source(h & 3, h >> 2)
            copy = remote(src, dst, recv, row, h, sent_all if apart else sent_not3)
            if apart:
                copy.start()
            else:
                pl.when(is3)(lambda: local(src, dst, recv))
                pl.when(jnp.logical_not(is3))(copy.start)

    def to_group(source, dst, recv):
        for apart in (2, 3, 1):
            w = lax.rem(member + apart, 4)
            remote(source(w), dst, recv, row, group * 4 + w, sent_all).start()
        local(source(member), dst, recv)

    def to_cols(targets, source, dst, recv):
        for to_col in targets:
            remote(source(to_col), dst, recv, row, to_col, sent3, lambda: source(0)).start()

    def to_rows(source, dst, recv, count):
        for apart in FAR_FIRST if count == 16 else (2, 3, 1):
            target = lax.rem(row + apart, 16) if count == 16 else (
                row_group * 4 + lax.rem(row_in + apart, 4)
            )
            remote(source(), dst, recv, target, col, sent3, source).start()
        local(source(), dst, recv)

    def lane_block(index):
        return pl.ds(pl.multiple_of(LANES * index, LANES), LANES)

    order = reversed_digits(iota((TOK, TOK), 0)) == iota((TOK, TOK), 1)
    permute = onehot(order)
    permute_scaled = onehot(order, SCALE)
    for load, table, src, dst in zip(
        loads,
        (permute_scaled, permute, permute, permute),
        (q_in, g_in, k_in, v_in),
        (qp, gp, kp, vp),
    ):
        load.wait()
        dst[...] = mm(table, src[...]).astype(BF16)

    low64 = iota((64, LANES), 1) < HEAD_DIM
    low256 = iota((TOK, LANES), 1) < HEAD_DIM

    for w in range(4):
        rows = slice(64 * w, 64 * w + 64)
        for i in range(3):
            tile = slice(LANES * (2 * i + w // 2), LANES * (2 * i + w // 2) + LANES)
            for slot, (first, second) in enumerate(((qp, gp), (kp, vp))):
                one = first[rows, tile].astype(F32)
                two = second[rows, tile].astype(F32)
                if w % 2 == 0:
                    two = swap(two)
                else:
                    one = swap(one)
                pack[w, i, slot] = jnp.where(low64, one, two).astype(BF16)

    pl.semaphore_wait(barrier, jnp.where(is3, 30, 15))

    to_workers(
        lambda w, i: pack.at[w, i, :, pl.ds(pl.multiple_of(16 * i, 16), 16), :],
        recv3.at[:, pl.ds(pl.multiple_of(16 * col, 16), 16), :], 1,
    )
    my_rows = pl.ds(pl.multiple_of(64 * member, 64), 64)
    to_group(lambda w: pack.at[w], recv_a.at[:, :, my_rows, :], 0)

    lane = iota((1, TOK), 1)
    src128 = iota((LANES, TOK), 0)
    dst128 = iota((LANES, TOK), 1)
    src256 = iota((TOK, TOK), 0)
    dst256 = iota((TOK, TOK), 1)
    both = jnp.logical_and
    start = 64 * lax.rem(member, 2) + 16 * group
    tab_a[...] = onehot(src128 == start + (dst128 & 15))
    tab_d[...] = onehot(src256 == 64 * ((dst256 >> 4) & 3) + 16 * group + (dst256 & 15))
    lane5 = both(src256 == 16 * (dst256 & 15), (dst256 >> 4) == lax.rem(row, 8))
    lane4 = both(
        src256 == 16 * ((dst256 >> 2) & 15) + (dst256 & 3),
        ((dst256 >> 6) & 1) == lax.rem(row_in, 2),
    )
    tab_out[...] = onehot(
        jnp.logical_or(both(lane5, dst256 < LANES), both(lane4, dst256 >= LANES))
    )
    tab_64[...] = onehot(src128 == 64 * lax.rem(member, 2) + (dst128 & 63))
    tab_16[...] = onehot(src128 == 16 * lax.rem(col, 8) + (dst128 & 15))
    tab_h[...] = onehot(
        src128 == 64 * lax.rem(group, 2) + 16 * (dst128 >> 6) + (dst128 & 15)
    )
    tab_p4[...] = onehot(
        iota((TOK, 64), 0) == 16 * (iota((TOK, 64), 1) >> 2) + (iota((TOK, 64), 1) & 3)
    )
    tab_p5[...] = onehot(iota((TOK, 16), 0) == 16 * iota((TOK, 16), 1))

    def pair_forward(j, carry):
        lanes = pl.ds(pl.multiple_of(j * LANES, LANES), LANES)
        q, k, v, g = qp[:, lanes], kp[:, lanes], vp[:, lanes], gp[:, lanes]
        zero = jnp.zeros_like(k)
        i = j // 2
        for parity in range(2):
            mine = low256 if parity == 0 else jnp.logical_not(low256)
            scores = mm_nt(jnp.where(mine, k, zero), q)
            dprob = mm_nt(jnp.where(mine, v, zero), g)
            weights, stat = forward(scores, dprob)
            w_all[2 * j + parity] = weights
            d_all[2 * j + parity] = dprob
            st1[2 * lax.rem(j, 2) + parity, i] = stat
        return carry

    def packed_forward(query_side, key_side, unit):
        zero = jnp.zeros_like(key_side)
        scores = mm_nt(jnp.where(low256, key_side, zero), query_side)
        dprob = mm_nt(jnp.where(low256, zero, key_side), query_side)
        weights, stat = forward(scores, dprob)
        w_all[unit] = weights
        d_all[unit] = dprob
        return stat

    lax.fori_loop(0, PAIRS, pair_forward, 0)

    rows4 = pl.ds(pl.multiple_of(64 * row_in, 64), 64)
    rows5 = pl.ds(pl.multiple_of(16 * row, 16), 16)

    @pl.when(is3)
    def _():
        pick4 = onehot(
            iota((64, TOK), 1) == 16 * (iota((64, TOK), 0) >> 2) + (iota((64, TOK), 0) & 3)
        )
        pick5 = onehot(iota((16, TOK), 1) == 16 * iota((16, TOK), 0))
        arrive(recv3, 1)
        sel5[1] = mm(pick5, recv3[1]).astype(BF16)
        sel4[1] = mm(pick4, recv3[1]).astype(BF16)
        to_rows(lambda: sel5.at[1], recv5.at[1, rows5, :], 7, 16)
        to_rows(lambda: sel4.at[1], recv4.at[1, rows4, :], 6, 4)
        sel5[0] = mm(pick5, recv3[0]).astype(BF16)
        sel4[0] = mm(pick4, recv3[0]).astype(BF16)

    to_workers(lambda w, i: st1.at[w, i, :, lane_block(w >> 1)], a_own.at[col], 2)
    to_group(lambda w: st1.at[w, :, :, lane_block(w >> 1)], b_own.at[member], 3)

    arrive(recv_a, 0)
    for i in range(3):
        st2[i] = packed_forward(recv_a[i, 0], recv_a[i, 1], HEADS + i)
    for apart in range(3):
        i = lax.rem(group + apart, 3)
        copy = remote(
            st2.at[i], d_two.at[group], 5, row, member + 4 * i, sent_all if apart else sent_not3
        )
        if apart:
            copy.start()
        else:
            pl.when(is3)(lambda: local(st2.at[group], d_two.at[group], 5))
            pl.when(jnp.logical_not(is3))(copy.start)
    to_group(lambda w: st2.at[:, :, lane_block(w >> 1)], c_two.at[member], 4)

    kept4 = (lane & 15) < 4
    kept5 = (lane & 15) == 0

    def picked(moved, count, hit):
        total = jnp.zeros((8, TOK), F32)
        for step in range(count):
            total = total + jnp.where(hit(step), moved[step], 0.0)
        return total

    @pl.when(is3)
    def _():
        to_rows(lambda: sel5.at[0], recv5.at[0, rows5, :], 13, 16)
        to_rows(lambda: sel4.at[0], recv4.at[0, rows4, :], 12, 4)

    @pl.when(is3)
    def _():
        st_l[0] = packed_forward(recv3[0], recv3[1], 15)
        arrive(a_own, 2)
        one = move(a_own[...].reshape(16 * 8, LANES), tab_a[...]).reshape(16, 8, TOK)
        one = rows_of(picked(one, 16, lambda c: (lane >> 4) == c))
        arrive(d_two, 5)
        two = move(d_two[...].reshape(4 * 8, TOK), tab_d[...]).reshape(4, 8, TOK)
        two = rows_of(picked(two, 4, lambda c: (lane >> 6) == c))
        early = merge([one, two, rows_of(st_l[0])])
        arrive(recv4.at[1], 6)
        st_l[1] = packed_forward(recv3[0], recv4[1], 16)
        arrive(recv5.at[1], 7)
        st_l[2] = packed_forward(recv3[0], recv5[1], 17)
        lse, delta = merge(
            [early, masked_rows(st_l[1], kept4), masked_rows(st_l[2], kept5)]
        )
        final = stat_tile(lse, delta, 0.0)
        st3[...] = final

        def block(to_col):
            return st3.at[:, lane_block(to_col >> 3)]

        to_cols(
            [4 * ((group + apart) & 3) + member for apart in range(1, 4)],
            block, h_three.at[group], 9,
        )
        local(block(col), h_three.at[group], 9)
        moved = move(final, tab_out[...])
        st5_out[...] = moved[0:2, :LANES]
        st4_out[...] = moved[0:2, LANES:]
        to_rows(lambda: st5_out, j_three.at[row], 11, 16)
        to_rows(lambda: st4_out, i_three.at[row_in], 10, 4)
        to_cols(
            [
                4 * ((group + apart) & 3) + ((member + beside) & 3)
                for beside in range(1, 4)
                for apart in range(4)
            ],
            block, g_three.at[member, group], 8,
        )

    def packed_backward(query_side, key_side, unit, stat, final):
        probs, dscore = backward(
            w_all[unit], d_all[unit], stat[2:3], final[0:1], final[1:2]
        )
        zero = jnp.zeros_like(key_side)
        both = mm(dscore, jnp.where(low256, query_side, zero)) + mm(
            probs, jnp.where(low256, zero, query_side)
        )
        return both, mm_tn(dscore, jnp.where(low256, key_side, zero))

    others_of_row = [lax.rem(col + apart, 16) for apart in range(1, 16)]

    def rows_of_owner(slot, to_col):
        return out_l.at[slot, pl.ds(pl.multiple_of(16 * to_col, 16), 16), :]

    def low_part(tile, low):
        return jnp.where(low, tile, jnp.zeros_like(tile))

    def high_part(tile, low):
        return jnp.where(low, jnp.zeros_like(tile), tile)

    @pl.when(is3)
    def _():
        pair3, own = packed_backward(recv3[0], recv3[1], 15, st_l[0], st3[...])
        base3[...] = pair3
        for unit, keys_of, kept in ((1, recv4, kept4), (2, recv5, kept5)):
            _, dscore = backward(
                w_all[15 + unit], d_all[15 + unit],
                jnp.where(kept, st_l[unit, 2:3], NEG_FILL), st3[0:1], st3[1:2],
            )
            own = own + mm_tn(dscore, low_part(keys_of[1], low256))
        out_l[1] = own.astype(BF16)
        to_cols(others_of_row, lambda to_col: rows_of_owner(1, to_col), back3.at[col, 1], 16)
        local(rows_of_owner(1, col), back3.at[col, 1], 16)
        arrive(recv4.at[0], 12)
        arrive(recv5.at[0], 13)
        for keyed, own_rows, others in ((keyed4, sel4, recv4), (keyed5, sel5, recv5)):
            low = iota(own_rows.shape[1:], 1) < HEAD_DIM
            keyed[0] = mm_nt(low_part(own_rows[1], low), others[0])
            keyed[1] = mm_nt(high_part(own_rows[1], low), others[0])

    arrive(b_own, 3)
    arrive(h_three, 9)
    local(h_three, g_three.at[member], 8)
    own2 = move(b_own[...].reshape(4 * 3 * 8, LANES), tab_64[...]).reshape(4, 3, 8, TOK)
    long2 = move(h_three[...].reshape(3 * 8, LANES), tab_h[...]).reshape(3, 8, TOK)
    for i in range(3):
        one = rows_of(picked(own2[:, i], 4, lambda c: (lane >> 6) == c))
        lse, delta = merge([one, rows_of(st2[i])])
        long = ((lane >> 4) & 3) == i
        fin2[i] = stat_tile(
            jnp.where(long, long2[i][0:1], lse), jnp.where(long, long2[i][1:2], delta), 0.0
        )

    swapped = []
    for i in range(3):
        pair, own = packed_backward(recv_a[i, 0], recv_a[i, 1], HEADS + i, st2[i], fin2[i])
        out2[i] = pair.astype(BF16)
        swapped.append(own)
    out2[3] = (swapped[0] + swap(swapped[1])).astype(BF16)
    out2[4] = swapped[2].astype(BF16)
    to_group(
        lambda w: out2.at[:, pl.ds(pl.multiple_of(64 * w, 64), 64), :], back2.at[member], 14
    )

    @pl.when(is3)
    def _():
        def keyed_backward(keyed, total, others):
            probs = jnp.exp(keyed[0] - total[0:1])
            dscore = probs * (keyed[1] - total[1:2])
            pair = mm(dscore.astype(BF16), low_part(others[0], low256)) + mm(
                probs.astype(BF16), high_part(others[0], low256)
            )
            return pair.astype(BF16)

        arrive(i_three, 10)
        total = jnp.concatenate([i_three[0] + i_three[1], i_three[2] + i_three[3]], axis=1)
        pair = base3[...] + mm(tab_p4[...], keyed_backward(keyed4, total, recv4))
        arrive(j_three, 11)
        halves = []
        for half in range(2):
            some = j_three[8 * half]
            for step in range(1, 8):
                some = some + j_three[8 * half + step]
            halves.append(some)
        total = jnp.concatenate(halves, axis=1)
        pair = pair + mm(tab_p5[...], keyed_backward(keyed5, total, recv5))
        out_l[0] = pair.astype(BF16)

        to_cols(others_of_row, lambda to_col: rows_of_owner(0, to_col), back3.at[col, 0], 15)
        local(rows_of_owner(0, col), back3.at[col, 0], 15)

    arrive(c_two, 4)
    arrive(g_three, 8)
    two1 = move(c_two[...].reshape(HEADS * 8, LANES), tab_64[...]).reshape(4, 3, 8, TOK)
    three1 = move(g_three[...].reshape(HEADS * 8, LANES), tab_16[...]).reshape(4, 3, 8, TOK)
    for h in range(HEADS):
        w, i = h % 4, h // 4
        one = rows_of(st1[w, i])
        lse, delta = merge([one, masked_rows(two1[w, i], (lane >> 6) == w)])
        long = (lane >> 4) == 4 * w + i
        fin1[h] = stat_tile(
            jnp.where(long, three1[w, i][0:1], lse), jnp.where(long, three1[w, i][1:2], delta), 0.0
        )

    def pair_backward(j, carry):
        lanes = pl.ds(pl.multiple_of(j * LANES, LANES), LANES)
        q, k, g = qp[:, lanes], kp[:, lanes], gp[:, lanes]
        zero = jnp.zeros_like(k)
        i = j // 2
        sum_q = sum_k = sum_v = 0.0
        for parity in range(2):
            mine = low256 if parity == 0 else jnp.logical_not(low256)
            h = 2 * j + parity
            stat = st1[2 * lax.rem(j, 2) + parity, i]
            final = fin1[h]
            probs, dscore = backward(w_all[h], d_all[h], stat[2:3], final[0:1], final[1:2])
            sum_v = sum_v + mm(probs, jnp.where(mine, g, zero))
            sum_k = sum_k + mm(dscore, jnp.where(mine, q, zero))
            sum_q = sum_q + mm_tn(dscore, jnp.where(mine, k, zero))
        acc_q[:, lanes] = sum_q
        acc_k[:, lanes] = sum_k
        acc_v[:, lanes] = sum_v
        return carry

    lax.fori_loop(0, PAIRS, pair_backward, 0)

    for left in sent_all:
        left()

    @pl.when(is3)
    def _():
        for left in sent3:
            left()

    @pl.when(jnp.logical_not(is3))
    def _():
        for left in sent_not3:
            left()

    def returned(w, count, pair, own, own_low):
        low = iota((count, LANES), 1) < HEAD_DIM
        pair = pair.astype(F32)
        own = own.astype(F32)
        other = swap(pair)
        if (w % 2 == 0) != own_low:
            own = swap(own)
        if w % 2 == 0:
            return [jnp.where(low, part, 0.0) for part in (own, pair, other)]
        return [jnp.where(low, 0.0, part) for part in (own, other, pair)]

    heads = [
        (h, h % 4, h // 4, slice(LANES * (h // 2), LANES * (h // 2) + LANES))
        for h in range(HEADS)
    ]
    sums = ((acc_q, sum_q), (acc_k, sum_k), (acc_v, sum_v))
    arrive(back2, 14)
    for h, w, i, tile in heads:
        rows = slice(64 * w, 64 * w + 64)
        parts = returned(w, 64, back2[w, i], back2[w, 3 + i // 2], i != 1)
        for part, (acc, _) in zip(parts, sums):
            acc[rows, tile] += part
    for acc, out in sums:
        out[...] = acc[...].astype(BF16)
    arrive(back3.at[:, 1], 16)
    arrive(back3.at[:, 0], 15)
    for h, w, i, tile in heads:
        rows = slice(64 * w + 16 * i, 64 * w + 16 * i + 16)
        parts = returned(w, 16, back3[h, 0], back3[h, 1], True)
        for part, (acc, out) in zip(parts, sums):
            out[rows, tile] = (acc[rows, tile] + part).astype(BF16)


def restore(sum_q, sum_k, sum_v, dq_hbm, dk_hbm, dv_hbm, dq, dk, dv, sems):
    order = reversed_digits(iota((TOK, TOK), 0)) == iota((TOK, TOK), 1)
    copies = []
    for slot, (src, tile, dst) in enumerate(
        ((sum_q, dq, dq_hbm), (sum_k, dk, dk_hbm), (sum_v, dv, dv_hbm))
    ):
        table = onehot(order, SCALE if slot == 0 else 1.0)
        tile[...] = mm(table, src[...]).astype(BF16)
        copy = pltpu.make_async_copy(tile, dst, sems.at[slot])
        copy.start()
        copies.append(copy)
    for copy in copies:
        copy.wait()


def body(queries, keys, values, grad_out):
    vm = pltpu.VMEM
    whole = pl.BlockSpec(memory_space=pltpu.VMEM)
    hbm = pl.BlockSpec(memory_space=pltpu.HBM)
    array = jax.ShapeDtypeStruct((TOK, WIDTH), BF16)
    queries, keys, values, grad_out = [
        pltpu.with_memory_space_constraint(x, pltpu.HBM) for x in (queries, keys, values, grad_out)
    ]
    sums = pl.pallas_call(
        kernel,
        out_shape=[array] * 3,
        in_specs=[hbm] * 4,
        out_specs=[whole] * 3,
        scratch_shapes=[vm((TOK, WIDTH), BF16)] * 8
        + [vm((TOK, WIDTH), F32)] * 3
        + [
            vm((18, TOK, TOK), F32),
            vm((18, TOK, TOK), F32),
            vm((4, 3, 2, 64, LANES), BF16),
            vm((3, 2, TOK, LANES), BF16),
            vm((2, TOK, LANES), BF16),
            vm((2, TOK, LANES), BF16),
            vm((2, TOK, LANES), BF16),
            vm((2, 64, LANES), BF16),
            vm((2, 16, LANES), BF16),
            vm((4, 3, 8, TOK), F32),
            vm((3, 8, TOK), F32),
            vm((3, 8, TOK), F32),
            vm((HEADS, 8, TOK), F32),
            vm((3, 8, TOK), F32),
            vm((8, TOK), F32),
            vm((2, LANES), F32),
            vm((2, LANES), F32),
            vm((16, 8, LANES), F32),
            vm((4, 3, 8, LANES), F32),
            vm((4, 3, 8, LANES), F32),
            vm((4, 8, TOK), F32),
            vm((4, 3, 8, LANES), F32),
            vm((3, 8, LANES), F32),
            vm((4, 2, LANES), F32),
            vm((16, 2, LANES), F32),
            vm((LANES, TOK), BF16),
            vm((TOK, TOK), BF16),
            vm((TOK, TOK), BF16),
            vm((LANES, TOK), BF16),
            vm((LANES, TOK), BF16),
            vm((LANES, TOK), BF16),
            vm((TOK, 64), BF16),
            vm((TOK, 16), BF16),
            vm((5, TOK, LANES), BF16),
            vm((2, TOK, LANES), BF16),
            vm((TOK, LANES), F32),
            vm((2, 64, TOK), F32),
            vm((2, 16, TOK), F32),
            vm((4, 5, 64, LANES), BF16),
            vm((HEADS, 2, 16, LANES), BF16),
            pltpu.SemaphoreType.DMA((144,)),
            pltpu.SemaphoreType.DMA((17,)),
            pltpu.SemaphoreType.DMA((4,)),
        ],
        compiler_params=pltpu.CompilerParams(
            collective_id=0, has_side_effects=True, vmem_limit_bytes=48 * 1024 * 1024
        ),
    )(queries, keys, values, grad_out)
    return pl.pallas_call(
        restore,
        out_shape=[array] * 3,
        in_specs=[whole] * 3,
        out_specs=[hbm] * 3,
        scratch_shapes=[vm((TOK, WIDTH), BF16)] * 3 + [pltpu.SemaphoreType.DMA((3,))],
        compiler_params=pltpu.CompilerParams(vmem_limit_bytes=16 * 1024 * 1024),
    )(*sums)


def solution(mesh):
    spec = P(("row", "col"), None)
    return jax.shard_map(
        body, mesh=mesh, in_specs=(spec,) * 4, out_specs=(spec,) * 3, check_vma=False
    )
```

```python
import jax
import jax.numpy as jnp
from jax import lax
from jax.experimental import pallas as pl
from jax.experimental.pallas import tpu as pltpu
from jax.sharding import PartitionSpec as P

HEADS = 12
HEAD_DIM = 64
TOK = 256
WIDTH = 768
LANES = 128
SCALE = HEAD_DIM**-0.5
NEG_FILL = -1e30
PAIRS = HEADS // 2
MESH = pl.DeviceIdType.MESH
FAR_FIRST = (8, 9, 7, 10, 6, 11, 5, 12, 4, 13, 3, 14, 2, 15, 1)
F32 = jnp.float32
BF16 = jnp.bfloat16


def mm(a, b):
    return lax.dot_general(a, b, (((1,), (0,)), ((), ())), preferred_element_type=F32)


def mm_nt(a, b):
    return lax.dot_general(a, b, (((1,), (1,)), ((), ())), preferred_element_type=F32)


def mm_tn(a, b):
    return lax.dot_general(a, b, (((0,), (0,)), ((), ())), preferred_element_type=F32)


def iota(shape, dim):
    return lax.broadcasted_iota(jnp.int32, shape, dim)


def onehot(hit, value=1.0):
    return jnp.where(hit, value, 0.0).astype(BF16)


def move(rows, table):
    count = rows.shape[0]
    high = rows.astype(BF16).astype(F32)
    rest = rows - high
    middle = rest.astype(BF16).astype(F32)
    parts = jnp.concatenate([high, middle, rest - middle], axis=0).astype(BF16)
    moved = mm(parts, table)
    return moved[:count] + moved[count : 2 * count] + moved[2 * count :]


def swap(tile):
    return pltpu.roll(tile, HEAD_DIM, 1)


def reversed_digits(index):
    return (index & 3) * 64 + ((index >> 2) & 3) * 16 + ((index >> 4) & 3) * 4 + (index >> 6)


def forward(scores, dprob):
    row_max = jnp.max(scores, axis=0, keepdims=True)
    weights = jnp.exp(scores - row_max)
    row_sum = jnp.sum(weights, axis=0, keepdims=True)
    dot_sum = jnp.sum(weights * dprob, axis=0, keepdims=True)
    return weights, stat_tile(row_max + jnp.log(row_sum), dot_sum / row_sum, row_max)


def stat_tile(lse, delta, row_max):
    row = iota((8, TOK), 0)
    return jnp.where(row == 0, lse, jnp.where(row == 1, delta, jnp.where(row == 2, row_max, 0.0)))


def backward(weights, dprob, row_max, lse, delta):
    probs = weights * jnp.exp(row_max - lse)
    dscore = probs * (dprob - delta)
    return probs.astype(BF16), dscore.astype(BF16)


def merge(parts):
    top = parts[0][0]
    for lse, _ in parts[1:]:
        top = jnp.maximum(top, lse)
    norm = 0.0
    total = 0.0
    for lse, delta in parts:
        factor = jnp.exp(lse - top)
        norm = norm + factor
        total = total + factor * delta
    return top + jnp.log(norm), total / norm


def rows_of(tile):
    return tile[0:1], tile[1:2]


def masked_rows(tile, hit):
    lse, delta = rows_of(tile)
    return jnp.where(hit, lse, NEG_FILL), jnp.where(hit, delta, 0.0)


def kernel(
    q_hbm, k_hbm, v_hbm, g_hbm, sum_q, sum_k, sum_v, order_out,
    q_in, k_in, v_in, g_in, qp, kp, vp, gp, acc_q, acc_k, acc_v,
    w_all, d_all, pack, recv_a, recv3, recv4, recv5, sel4, sel5,
    st1, st2, st_l, fin1, fin2, st3, st4_out, st5_out,
    a_own, b_own, c_two, d_two, g_three, h_three, i_three, j_three,
    tab_a, tab_d, tab_out, tab_64, tab_16, tab_h, tab_p4, tab_p5,
    out2, out_l, base3, keyed4, keyed5, back2, back3,
    send_sem, recv_sem, load_sem,
):
    row = lax.axis_index("row")
    col = lax.axis_index("col")
    member = lax.rem(col, 4)
    group = col // 4
    row_in = lax.rem(row, 4)
    row_group = row // 4
    is3 = col < HEADS

    loads = []
    for slot, (src, dst) in enumerate(
        ((q_hbm, q_in), (g_hbm, g_in), (k_hbm, k_in), (v_hbm, v_in))
    ):
        load = pltpu.make_async_copy(src, dst, load_sem.at[slot])
        load.start()
        loads.append(load)

    barrier = pltpu.get_barrier_semaphore()

    def greet(to_row, to_col):
        pl.semaphore_signal(barrier, inc=1, device_id=(to_row, to_col), device_id_type=MESH)

    @pl.when(is3)
    def _():
        for apart in FAR_FIRST:
            greet(lax.rem(row + apart, 16), col)

    for apart in range(1, 16):
        greet(row, lax.rem(col + apart, 16))

    slots = iter(range(144))
    sent_all, sent3, sent_not3 = [], [], []

    def remote(src, dst, recv, to_row, to_col, into, like=None):
        slot = next(slots)
        copy = pltpu.make_async_remote_copy(
            src_ref=src, dst_ref=dst, send_sem=send_sem.at[slot],
            recv_sem=recv_sem.at[recv], device_id=(to_row, to_col), device_id_type=MESH,
        )
        if like is None:
            into.append(copy.wait_send)
        else:
            into.append(lambda: pltpu.make_async_copy(like(), like(), send_sem.at[slot]).wait())
        return copy

    def local(src, dst, recv):
        pltpu.make_async_copy(src, dst, recv_sem.at[recv]).start()

    def arrive(buffer, recv):
        pltpu.make_async_copy(buffer, buffer, recv_sem.at[recv]).wait()

    def to_workers(source, dst, recv):
        base = jnp.where(is3, col, 3 * (col - HEADS))
        for apart in range(HEADS):
            h = lax.rem(base + apart, HEADS)
            src = source(h & 3, h >> 2)
            copy = remote(src, dst, recv, row, h, sent_all if apart else sent_not3)
            if apart:
                copy.start()
            else:
                pl.when(is3)(lambda: local(src, dst, recv))
                pl.when(jnp.logical_not(is3))(copy.start)

    def to_group(source, dst, recv):
        for apart in (2, 3, 1):
            w = lax.rem(member + apart, 4)
            remote(source(w), dst, recv, row, group * 4 + w, sent_all).start()
        local(source(member), dst, recv)

    def to_cols(targets, source, dst, recv):
        for to_col in targets:
            remote(source(to_col), dst, recv, row, to_col, sent3, lambda: source(0)).start()

    def to_rows(source, dst, recv, count):
        for apart in FAR_FIRST if count == 16 else (2, 3, 1):
            target = lax.rem(row + apart, 16) if count == 16 else (
                row_group * 4 + lax.rem(row_in + apart, 4)
            )
            remote(source(), dst, recv, target, col, sent3, source).start()
        local(source(), dst, recv)

    def lane_block(index):
        return pl.ds(pl.multiple_of(LANES * index, LANES), LANES)

    order = reversed_digits(iota((TOK, TOK), 0)) == iota((TOK, TOK), 1)
    permute = onehot(order)
    permute_scaled = onehot(order, SCALE)
    order_out[...] = permute
    for load, table, src, dst in zip(
        loads,
        (permute_scaled, permute, permute, permute),
        (q_in, g_in, k_in, v_in),
        (qp, gp, kp, vp),
    ):
        load.wait()
        dst[...] = mm(table, src[...]).astype(BF16)

    low64 = iota((64, LANES), 1) < HEAD_DIM
    low256 = iota((TOK, LANES), 1) < HEAD_DIM

    for w in range(4):
        rows = slice(64 * w, 64 * w + 64)
        for i in range(3):
            tile = slice(LANES * (2 * i + w // 2), LANES * (2 * i + w // 2) + LANES)
            for slot, (first, second) in enumerate(((qp, gp), (kp, vp))):
                one = first[rows, tile].astype(F32)
                two = second[rows, tile].astype(F32)
                if w % 2 == 0:
                    two = swap(two)
                else:
                    one = swap(one)
                pack[w, i, slot] = jnp.where(low64, one, two).astype(BF16)

    pl.semaphore_wait(barrier, jnp.where(is3, 30, 15))

    to_workers(
        lambda w, i: pack.at[w, i, :, pl.ds(pl.multiple_of(16 * i, 16), 16), :],
        recv3.at[:, pl.ds(pl.multiple_of(16 * col, 16), 16), :], 1,
    )
    my_rows = pl.ds(pl.multiple_of(64 * member, 64), 64)
    to_group(lambda w: pack.at[w], recv_a.at[:, :, my_rows, :], 0)

    lane = iota((1, TOK), 1)
    src128 = iota((LANES, TOK), 0)
    dst128 = iota((LANES, TOK), 1)
    src256 = iota((TOK, TOK), 0)
    dst256 = iota((TOK, TOK), 1)
    both = jnp.logical_and
    start = 64 * lax.rem(member, 2) + 16 * group
    tab_a[...] = onehot(src128 == start + (dst128 & 15))
    tab_d[...] = onehot(src256 == 64 * ((dst256 >> 4) & 3) + 16 * group + (dst256 & 15))
    lane5 = both(src256 == 16 * (dst256 & 15), (dst256 >> 4) == lax.rem(row, 8))
    lane4 = both(
        src256 == 16 * ((dst256 >> 2) & 15) + (dst256 & 3),
        ((dst256 >> 6) & 1) == lax.rem(row_in, 2),
    )
    tab_out[...] = onehot(
        jnp.logical_or(both(lane5, dst256 < LANES), both(lane4, dst256 >= LANES))
    )
    tab_64[...] = onehot(src128 == 64 * lax.rem(member, 2) + (dst128 & 63))
    tab_16[...] = onehot(src128 == 16 * lax.rem(col, 8) + (dst128 & 15))
    tab_h[...] = onehot(
        src128 == 64 * lax.rem(group, 2) + 16 * (dst128 >> 6) + (dst128 & 15)
    )
    tab_p4[...] = onehot(
        iota((TOK, 64), 0) == 16 * (iota((TOK, 64), 1) >> 2) + (iota((TOK, 64), 1) & 3)
    )
    tab_p5[...] = onehot(iota((TOK, 16), 0) == 16 * iota((TOK, 16), 1))

    def pair_forward(j, carry):
        lanes = pl.ds(pl.multiple_of(j * LANES, LANES), LANES)
        q, k, v, g = qp[:, lanes], kp[:, lanes], vp[:, lanes], gp[:, lanes]
        zero = jnp.zeros_like(k)
        i = j // 2
        for parity in range(2):
            mine = low256 if parity == 0 else jnp.logical_not(low256)
            scores = mm_nt(jnp.where(mine, k, zero), q)
            dprob = mm_nt(jnp.where(mine, v, zero), g)
            weights, stat = forward(scores, dprob)
            w_all[2 * j + parity] = weights
            d_all[2 * j + parity] = dprob
            st1[2 * lax.rem(j, 2) + parity, i] = stat
        return carry

    def packed_forward(query_side, key_side, unit):
        zero = jnp.zeros_like(key_side)
        scores = mm_nt(jnp.where(low256, key_side, zero), query_side)
        dprob = mm_nt(jnp.where(low256, zero, key_side), query_side)
        weights, stat = forward(scores, dprob)
        w_all[unit] = weights
        d_all[unit] = dprob
        return stat

    lax.fori_loop(0, PAIRS, pair_forward, 0)

    rows4 = pl.ds(pl.multiple_of(64 * row_in, 64), 64)
    rows5 = pl.ds(pl.multiple_of(16 * row, 16), 16)

    @pl.when(is3)
    def _():
        pick4 = onehot(
            iota((64, TOK), 1) == 16 * (iota((64, TOK), 0) >> 2) + (iota((64, TOK), 0) & 3)
        )
        pick5 = onehot(iota((16, TOK), 1) == 16 * iota((16, TOK), 0))
        arrive(recv3, 1)
        sel5[1] = mm(pick5, recv3[1]).astype(BF16)
        sel4[1] = mm(pick4, recv3[1]).astype(BF16)
        to_rows(lambda: sel5.at[1], recv5.at[1, rows5, :], 7, 16)
        to_rows(lambda: sel4.at[1], recv4.at[1, rows4, :], 6, 4)
        sel5[0] = mm(pick5, recv3[0]).astype(BF16)
        sel4[0] = mm(pick4, recv3[0]).astype(BF16)

    to_workers(lambda w, i: st1.at[w, i, :, lane_block(w >> 1)], a_own.at[col], 2)
    to_group(lambda w: st1.at[w, :, :, lane_block(w >> 1)], b_own.at[member], 3)

    arrive(recv_a, 0)
    for i in range(3):
        st2[i] = packed_forward(recv_a[i, 0], recv_a[i, 1], HEADS + i)
    for apart in range(3):
        i = lax.rem(group + apart, 3)
        copy = remote(
            st2.at[i], d_two.at[group], 5, row, member + 4 * i, sent_all if apart else sent_not3
        )
        if apart:
            copy.start()
        else:
            pl.when(is3)(lambda: local(st2.at[group], d_two.at[group], 5))
            pl.when(jnp.logical_not(is3))(copy.start)
    to_group(lambda w: st2.at[:, :, lane_block(w >> 1)], c_two.at[member], 4)

    kept4 = (lane & 15) < 4
    kept5 = (lane & 15) == 0

    def picked(moved, count, hit):
        total = jnp.zeros((8, TOK), F32)
        for step in range(count):
            total = total + jnp.where(hit(step), moved[step], 0.0)
        return total

    @pl.when(is3)
    def _():
        to_rows(lambda: sel5.at[0], recv5.at[0, rows5, :], 13, 16)
        to_rows(lambda: sel4.at[0], recv4.at[0, rows4, :], 12, 4)

    @pl.when(is3)
    def _():
        st_l[0] = packed_forward(recv3[0], recv3[1], 15)
        arrive(a_own, 2)
        arrive(d_two, 5)
        one = move(a_own[...].reshape(16 * 8, LANES), tab_a[...]).reshape(16, 8, TOK)
        one = rows_of(picked(one, 16, lambda c: (lane >> 4) == c))
        two = move(d_two[...].reshape(4 * 8, TOK), tab_d[...]).reshape(4, 8, TOK)
        two = rows_of(picked(two, 4, lambda c: (lane >> 6) == c))
        early = merge([one, two, rows_of(st_l[0])])
        arrive(recv4.at[1], 6)
        arrive(recv5.at[1], 7)
        st_l[1] = packed_forward(recv3[0], recv4[1], 16)
        st_l[2] = packed_forward(recv3[0], recv5[1], 17)
        lse, delta = merge(
            [early, masked_rows(st_l[1], kept4), masked_rows(st_l[2], kept5)]
        )
        final = stat_tile(lse, delta, 0.0)
        st3[...] = final

        def block(to_col):
            return st3.at[:, lane_block(to_col >> 3)]

        moved = move(final, tab_out[...])
        st5_out[...] = moved[0:2, :LANES]
        st4_out[...] = moved[0:2, LANES:]
        to_rows(lambda: st5_out, j_three.at[row], 11, 16)
        to_rows(lambda: st4_out, i_three.at[row_in], 10, 4)
        to_cols(
            [4 * ((group + apart) & 3) + member for apart in range(1, 4)],
            block, h_three.at[group], 9,
        )
        local(block(col), h_three.at[group], 9)
        to_cols(
            [
                4 * ((group + apart) & 3) + ((member + beside) & 3)
                for beside in range(1, 4)
                for apart in range(4)
            ],
            block, g_three.at[member, group], 8,
        )

    def packed_backward(query_side, key_side, unit, stat, final):
        probs, dscore = backward(
            w_all[unit], d_all[unit], stat[2:3], final[0:1], final[1:2]
        )
        zero = jnp.zeros_like(key_side)
        both = mm(dscore, jnp.where(low256, query_side, zero)) + mm(
            probs, jnp.where(low256, zero, query_side)
        )
        return both, mm_tn(dscore, jnp.where(low256, key_side, zero))

    others_of_row = [lax.rem(col + apart, 16) for apart in range(1, 16)]

    def rows_of_owner(slot, to_col):
        return out_l.at[slot, pl.ds(pl.multiple_of(16 * to_col, 16), 16), :]

    def low_part(tile, low):
        return jnp.where(low, tile, jnp.zeros_like(tile))

    def high_part(tile, low):
        return jnp.where(low, jnp.zeros_like(tile), tile)

    @pl.when(is3)
    def _():
        pair3, own = packed_backward(recv3[0], recv3[1], 15, st_l[0], st3[...])
        base3[...] = pair3
        for unit, keys_of, kept in ((1, recv4, kept4), (2, recv5, kept5)):
            _, dscore = backward(
                w_all[15 + unit], d_all[15 + unit],
                jnp.where(kept, st_l[unit, 2:3], NEG_FILL), st3[0:1], st3[1:2],
            )
            own = own + mm_tn(dscore, low_part(keys_of[1], low256))
        out_l[1] = own.astype(BF16)
        to_cols(others_of_row, lambda to_col: rows_of_owner(1, to_col), back3.at[col, 1], 16)
        local(rows_of_owner(1, col), back3.at[col, 1], 16)
        arrive(recv4.at[0], 12)
        arrive(recv5.at[0], 13)
        for keyed, own_rows, others in ((keyed4, sel4, recv4), (keyed5, sel5, recv5)):
            low = iota(own_rows.shape[1:], 1) < HEAD_DIM
            keyed[0] = mm_nt(low_part(own_rows[1], low), others[0])
            keyed[1] = mm_nt(high_part(own_rows[1], low), others[0])

    arrive(b_own, 3)
    arrive(h_three, 9)
    local(h_three, g_three.at[member], 8)
    own2 = move(b_own[...].reshape(4 * 3 * 8, LANES), tab_64[...]).reshape(4, 3, 8, TOK)
    long2 = move(h_three[...].reshape(3 * 8, LANES), tab_h[...]).reshape(3, 8, TOK)
    for i in range(3):
        one = rows_of(picked(own2[:, i], 4, lambda c: (lane >> 6) == c))
        lse, delta = merge([one, rows_of(st2[i])])
        long = ((lane >> 4) & 3) == i
        fin2[i] = stat_tile(
            jnp.where(long, long2[i][0:1], lse), jnp.where(long, long2[i][1:2], delta), 0.0
        )

    swapped = []
    for i in range(3):
        pair, own = packed_backward(recv_a[i, 0], recv_a[i, 1], HEADS + i, st2[i], fin2[i])
        out2[i] = pair.astype(BF16)
        swapped.append(own)
    out2[3] = (swapped[0] + swap(swapped[1])).astype(BF16)
    out2[4] = swapped[2].astype(BF16)
    @pl.when(is3)
    def _():
        def keyed_backward(keyed, total, others):
            probs = jnp.exp(keyed[0] - total[0:1])
            dscore = probs * (keyed[1] - total[1:2])
            pair = mm(dscore.astype(BF16), low_part(others[0], low256)) + mm(
                probs.astype(BF16), high_part(others[0], low256)
            )
            return pair.astype(BF16)

        arrive(i_three, 10)
        arrive(j_three, 11)
        total4 = jnp.concatenate([i_three[0] + i_three[1], i_three[2] + i_three[3]], axis=1)
        total5 = jnp.concatenate(
            [jnp.sum(j_three[0:8], axis=0), jnp.sum(j_three[8:16], axis=0)], axis=1
        )
        pair = (
            base3[...]
            + mm(tab_p4[...], keyed_backward(keyed4, total4, recv4))
            + mm(tab_p5[...], keyed_backward(keyed5, total5, recv5))
        )
        out_l[0] = pair.astype(BF16)

        to_cols(others_of_row, lambda to_col: rows_of_owner(0, to_col), back3.at[col, 0], 15)
        local(rows_of_owner(0, col), back3.at[col, 0], 15)

    to_group(
        lambda w: out2.at[:, pl.ds(pl.multiple_of(64 * w, 64), 64), :], back2.at[member], 14
    )

    arrive(c_two, 4)
    arrive(g_three, 8)
    two1 = move(c_two[...].reshape(HEADS * 8, LANES), tab_64[...]).reshape(4, 3, 8, TOK)
    three1 = move(g_three[...].reshape(HEADS * 8, LANES), tab_16[...]).reshape(4, 3, 8, TOK)
    for h in range(HEADS):
        w, i = h % 4, h // 4
        one = rows_of(st1[w, i])
        lse, delta = merge([one, masked_rows(two1[w, i], (lane >> 6) == w)])
        long = (lane >> 4) == 4 * w + i
        fin1[h] = stat_tile(
            jnp.where(long, three1[w, i][0:1], lse), jnp.where(long, three1[w, i][1:2], delta), 0.0
        )

    def pair_backward(j, carry):
        lanes = pl.ds(pl.multiple_of(j * LANES, LANES), LANES)
        q, k, g = qp[:, lanes], kp[:, lanes], gp[:, lanes]
        zero = jnp.zeros_like(k)
        i = j // 2
        sum_q = sum_k = sum_v = 0.0
        for parity in range(2):
            mine = low256 if parity == 0 else jnp.logical_not(low256)
            h = 2 * j + parity
            stat = st1[2 * lax.rem(j, 2) + parity, i]
            final = fin1[h]
            probs, dscore = backward(w_all[h], d_all[h], stat[2:3], final[0:1], final[1:2])
            sum_v = sum_v + mm(probs, jnp.where(mine, g, zero))
            sum_k = sum_k + mm(dscore, jnp.where(mine, q, zero))
            sum_q = sum_q + mm_tn(dscore, jnp.where(mine, k, zero))
        acc_q[:, lanes] = sum_q
        acc_k[:, lanes] = sum_k
        acc_v[:, lanes] = sum_v
        return carry

    lax.fori_loop(0, PAIRS, pair_backward, 0)

    for left in sent_all:
        left()

    @pl.when(is3)
    def _():
        for left in sent3:
            left()

    @pl.when(jnp.logical_not(is3))
    def _():
        for left in sent_not3:
            left()

    def returned(w, count, pair, own, own_low):
        low = iota((count, LANES), 1) < HEAD_DIM
        pair = pair.astype(F32)
        own = own.astype(F32)
        other = swap(pair)
        if (w % 2 == 0) != own_low:
            own = swap(own)
        if w % 2 == 0:
            return [jnp.where(low, part, 0.0) for part in (own, pair, other)]
        return [jnp.where(low, 0.0, part) for part in (own, other, pair)]

    heads = [
        (h, h % 4, h // 4, slice(LANES * (h // 2), LANES * (h // 2) + LANES))
        for h in range(HEADS)
    ]
    sums = ((acc_q, sum_q), (acc_k, sum_k), (acc_v, sum_v))
    arrive(back2, 14)
    for h, w, i, tile in heads:
        rows = slice(64 * w, 64 * w + 64)
        parts = returned(w, 64, back2[w, i], back2[w, 3 + i // 2], i != 1)
        for part, (acc, _) in zip(parts, sums):
            acc[rows, tile] += part
    for (acc, out), factor in zip(sums, (SCALE, 1.0, 1.0)):
        out[...] = (acc[...] * factor).astype(BF16)
    arrive(back3.at[:, 1], 16)
    arrive(back3.at[:, 0], 15)
    for h, w, i, tile in heads:
        rows = slice(64 * w + 16 * i, 64 * w + 16 * i + 16)
        parts = returned(w, 16, back3[h, 0], back3[h, 1], True)
        for part, (acc, out), factor in zip(parts, sums, (SCALE, 1.0, 1.0)):
            out[rows, tile] = ((acc[rows, tile] + part) * factor).astype(BF16)


def restore(sum_q, sum_k, sum_v, order, dq_hbm, dk_hbm, dv_hbm, dq, dk, dv, sems):
    copies = []
    for slot, (src, tile, dst) in enumerate(
        ((sum_q, dq, dq_hbm), (sum_k, dk, dk_hbm), (sum_v, dv, dv_hbm))
    ):
        tile[...] = mm(order[...], src[...]).astype(BF16)
        copy = pltpu.make_async_copy(tile, dst, sems.at[slot])
        copy.start()
        copies.append(copy)
    for copy in copies:
        copy.wait()


def body(queries, keys, values, grad_out):
    vm = pltpu.VMEM
    whole = pl.BlockSpec(memory_space=pltpu.VMEM)
    hbm = pl.BlockSpec(memory_space=pltpu.HBM)
    array = jax.ShapeDtypeStruct((TOK, WIDTH), BF16)
    queries, keys, values, grad_out = [
        pltpu.with_memory_space_constraint(x, pltpu.HBM) for x in (queries, keys, values, grad_out)
    ]
    sums = pl.pallas_call(
        kernel,
        out_shape=[array] * 3 + [jax.ShapeDtypeStruct((TOK, TOK), BF16)],
        in_specs=[hbm] * 4,
        out_specs=[whole] * 4,
        scratch_shapes=[vm((TOK, WIDTH), BF16)] * 8
        + [vm((TOK, WIDTH), F32)] * 3
        + [
            vm((18, TOK, TOK), F32),
            vm((18, TOK, TOK), F32),
            vm((4, 3, 2, 64, LANES), BF16),
            vm((3, 2, TOK, LANES), BF16),
            vm((2, TOK, LANES), BF16),
            vm((2, TOK, LANES), BF16),
            vm((2, TOK, LANES), BF16),
            vm((2, 64, LANES), BF16),
            vm((2, 16, LANES), BF16),
            vm((4, 3, 8, TOK), F32),
            vm((3, 8, TOK), F32),
            vm((3, 8, TOK), F32),
            vm((HEADS, 8, TOK), F32),
            vm((3, 8, TOK), F32),
            vm((8, TOK), F32),
            vm((2, LANES), F32),
            vm((2, LANES), F32),
            vm((16, 8, LANES), F32),
            vm((4, 3, 8, LANES), F32),
            vm((4, 3, 8, LANES), F32),
            vm((4, 8, TOK), F32),
            vm((4, 3, 8, LANES), F32),
            vm((3, 8, LANES), F32),
            vm((4, 2, LANES), F32),
            vm((16, 2, LANES), F32),
            vm((LANES, TOK), BF16),
            vm((TOK, TOK), BF16),
            vm((TOK, TOK), BF16),
            vm((LANES, TOK), BF16),
            vm((LANES, TOK), BF16),
            vm((LANES, TOK), BF16),
            vm((TOK, 64), BF16),
            vm((TOK, 16), BF16),
            vm((5, TOK, LANES), BF16),
            vm((2, TOK, LANES), BF16),
            vm((TOK, LANES), F32),
            vm((2, 64, TOK), F32),
            vm((2, 16, TOK), F32),
            vm((4, 5, 64, LANES), BF16),
            vm((HEADS, 2, 16, LANES), BF16),
            pltpu.SemaphoreType.DMA((144,)),
            pltpu.SemaphoreType.DMA((17,)),
            pltpu.SemaphoreType.DMA((4,)),
        ],
        compiler_params=pltpu.CompilerParams(
            collective_id=0, has_side_effects=True, vmem_limit_bytes=48 * 1024 * 1024
        ),
    )(queries, keys, values, grad_out)
    return pl.pallas_call(
        restore,
        out_shape=[array] * 3,
        in_specs=[whole] * 4,
        out_specs=[hbm] * 3,
        scratch_shapes=[vm((TOK, WIDTH), BF16)] * 3 + [pltpu.SemaphoreType.DMA((3,))],
        compiler_params=pltpu.CompilerParams(vmem_limit_bytes=16 * 1024 * 1024),
    )(*sums)


def solution(mesh):
    spec = P(("row", "col"), None)
    return jax.shard_map(
        body, mesh=mesh, in_specs=(spec,) * 4, out_specs=(spec,) * 3, check_vma=False
    )
```

```python
import jax
import jax.numpy as jnp
from jax import lax
from jax.experimental import pallas as pl
from jax.experimental.pallas import tpu as pltpu
from jax.sharding import PartitionSpec as P

HEADS = 12
HEAD_DIM = 64
TOK = 256
WIDTH = 768
LANES = 128
SCALE = HEAD_DIM**-0.5
NEG_FILL = -1e30
PAIRS = HEADS // 2
MESH = pl.DeviceIdType.MESH
FAR_FIRST = (8, 9, 7, 10, 6, 11, 5, 12, 4, 13, 3, 14, 2, 15, 1)
F32 = jnp.float32
BF16 = jnp.bfloat16


def mm(a, b):
    return lax.dot_general(a, b, (((1,), (0,)), ((), ())), preferred_element_type=F32)


def mm_nt(a, b):
    return lax.dot_general(a, b, (((1,), (1,)), ((), ())), preferred_element_type=F32)


def mm_tn(a, b):
    return lax.dot_general(a, b, (((0,), (0,)), ((), ())), preferred_element_type=F32)


def iota(shape, dim):
    return lax.broadcasted_iota(jnp.int32, shape, dim)


def onehot(hit, value=1.0):
    return jnp.where(hit, value, 0.0).astype(BF16)


def move(rows, table):
    count = rows.shape[0]
    high = rows.astype(BF16).astype(F32)
    rest = rows - high
    middle = rest.astype(BF16).astype(F32)
    parts = jnp.concatenate([high, middle, rest - middle], axis=0).astype(BF16)
    moved = mm(parts, table)
    return moved[:count] + moved[count : 2 * count] + moved[2 * count :]


def swap(tile):
    return pltpu.roll(tile, HEAD_DIM, 1)


def reversed_digits(index):
    return (index & 3) * 64 + ((index >> 2) & 3) * 16 + ((index >> 4) & 3) * 4 + (index >> 6)


def forward(scores, dprob):
    row_max = jnp.max(scores, axis=0, keepdims=True)
    weights = jnp.exp(scores - row_max)
    row_sum = jnp.sum(weights, axis=0, keepdims=True)
    dot_sum = jnp.sum(weights * dprob, axis=0, keepdims=True)
    return weights, stat_tile(row_max + jnp.log(row_sum), dot_sum / row_sum, row_max)


def stat_tile(lse, delta, row_max):
    row = iota((8, TOK), 0)
    return jnp.where(row == 0, lse, jnp.where(row == 1, delta, jnp.where(row == 2, row_max, 0.0)))


def backward(weights, dprob, row_max, lse, delta):
    probs = weights * jnp.exp(row_max - lse)
    dscore = probs * (dprob - delta)
    return probs.astype(BF16), dscore.astype(BF16)


def merge(parts):
    top = parts[0][0]
    for lse, _ in parts[1:]:
        top = jnp.maximum(top, lse)
    norm = 0.0
    total = 0.0
    for lse, delta in parts:
        factor = jnp.exp(lse - top)
        norm = norm + factor
        total = total + factor * delta
    return top + jnp.log(norm), total / norm


def rows_of(tile):
    return tile[0:1], tile[1:2]


def masked_rows(tile, hit):
    lse, delta = rows_of(tile)
    return jnp.where(hit, lse, NEG_FILL), jnp.where(hit, delta, 0.0)


def kernel(
    q_hbm, k_hbm, v_hbm, g_hbm, sum_q, sum_k, sum_v, order_out,
    q_in, k_in, v_in, g_in, qp, kp, vp, gp, acc_q, acc_k, acc_v,
    w_all, d_all, pack, recv_a, recv3, recv4, recv5, sel4, sel5,
    st1, st2, st_l, fin1, fin2, st3, st4_out, st5_out,
    a_own, b_own, c_two, d_two, g_three, h_three, i_three, j_three,
    tab_a, tab_d, tab_out, tab_64, tab_16, tab_h, tab_p4, tab_p5,
    out2, out_l, base3, keyed4, keyed5, back2, back3,
    send_sem, recv_sem, load_sem,
):
    row = lax.axis_index("row")
    col = lax.axis_index("col")
    member = lax.rem(col, 4)
    group = col // 4
    row_in = lax.rem(row, 4)
    row_group = row // 4
    is3 = col < HEADS

    loads = []
    for slot, (src, dst) in enumerate(
        ((q_hbm, q_in), (g_hbm, g_in), (k_hbm, k_in), (v_hbm, v_in))
    ):
        load = pltpu.make_async_copy(src, dst, load_sem.at[slot])
        load.start()
        loads.append(load)

    barrier = pltpu.get_barrier_semaphore()

    def greet(to_row, to_col):
        pl.semaphore_signal(barrier, inc=1, device_id=(to_row, to_col), device_id_type=MESH)

    @pl.when(is3)
    def _():
        for apart in FAR_FIRST:
            greet(lax.rem(row + apart, 16), col)

    for apart in range(1, 16):
        greet(row, lax.rem(col + apart, 16))

    slots = iter(range(160))
    sent_all, sent3, sent_not3 = [], [], []

    def remote(src, dst, recv, to_row, to_col, into, like=None):
        slot = next(slots)
        copy = pltpu.make_async_remote_copy(
            src_ref=src, dst_ref=dst, send_sem=send_sem.at[slot],
            recv_sem=recv_sem.at[recv], device_id=(to_row, to_col), device_id_type=MESH,
        )
        if like is None:
            into.append(copy.wait_send)
        else:
            into.append(lambda: pltpu.make_async_copy(like(), like(), send_sem.at[slot]).wait())
        return copy

    def local(src, dst, recv):
        pltpu.make_async_copy(src, dst, recv_sem.at[recv]).start()

    def arrive(buffer, recv):
        pltpu.make_async_copy(buffer, buffer, recv_sem.at[recv]).wait()

    def to_workers(source, dst, recv):
        base = jnp.where(is3, col, 3 * (col - HEADS))
        for apart in range(HEADS):
            h = lax.rem(base + apart, HEADS)
            src = source(h & 3, h >> 2)
            copy = remote(src, dst, recv, row, h, sent_all if apart else sent_not3)
            if apart:
                copy.start()
            else:
                pl.when(is3)(lambda: local(src, dst, recv))
                pl.when(jnp.logical_not(is3))(copy.start)

    def to_group(source, dst, recv):
        for apart in (2, 3, 1):
            w = lax.rem(member + apart, 4)
            remote(source(w), dst, recv, row, group * 4 + w, sent_all).start()
        local(source(member), dst, recv)

    def to_cols(targets, source, dst, recv):
        for to_col in targets:
            remote(source(to_col), dst, recv, row, to_col, sent3, lambda: source(0)).start()

    def to_rows(source, dst, recv, count):
        for apart in FAR_FIRST if count == 16 else (2, 3, 1):
            target = lax.rem(row + apart, 16) if count == 16 else (
                row_group * 4 + lax.rem(row_in + apart, 4)
            )
            remote(source(), dst, recv, target, col, sent3, source).start()
        local(source(), dst, recv)

    def lane_block(index):
        return pl.ds(pl.multiple_of(LANES * index, LANES), LANES)

    order = reversed_digits(iota((TOK, TOK), 0)) == iota((TOK, TOK), 1)
    permute = onehot(order)
    permute_scaled = onehot(order, SCALE)
    order_out[...] = permute
    for load, table, src, dst in zip(
        loads,
        (permute_scaled, permute, permute, permute),
        (q_in, g_in, k_in, v_in),
        (qp, gp, kp, vp),
    ):
        load.wait()
        dst[...] = mm(table, src[...]).astype(BF16)

    low64 = iota((64, LANES), 1) < HEAD_DIM
    low256 = iota((TOK, LANES), 1) < HEAD_DIM

    for w in range(4):
        rows = slice(64 * w, 64 * w + 64)
        for i in range(3):
            tile = slice(LANES * (2 * i + w // 2), LANES * (2 * i + w // 2) + LANES)
            for slot, (first, second) in enumerate(((qp, gp), (kp, vp))):
                one = first[rows, tile].astype(F32)
                two = second[rows, tile].astype(F32)
                if w % 2 == 0:
                    two = swap(two)
                else:
                    one = swap(one)
                pack[w, i, slot] = jnp.where(low64, one, two).astype(BF16)

    pl.semaphore_wait(barrier, jnp.where(is3, 30, 15))

    to_workers(
        lambda w, i: pack.at[w, i, :, pl.ds(pl.multiple_of(16 * i, 16), 16), :],
        recv3.at[:, pl.ds(pl.multiple_of(16 * col, 16), 16), :], 1,
    )
    my_rows = pl.ds(pl.multiple_of(64 * member, 64), 64)
    to_group(lambda w: pack.at[w], recv_a.at[:, :, my_rows, :], 0)

    lane = iota((1, TOK), 1)
    src128 = iota((LANES, TOK), 0)
    dst128 = iota((LANES, TOK), 1)
    src256 = iota((TOK, TOK), 0)
    dst256 = iota((TOK, TOK), 1)
    both = jnp.logical_and
    start = 64 * lax.rem(member, 2) + 16 * group
    tab_a[...] = onehot(src128 == start + (dst128 & 15))
    tab_d[...] = onehot(src256 == 64 * ((dst256 >> 4) & 3) + 16 * group + (dst256 & 15))
    lane5 = both(src256 == 16 * (dst256 & 15), (dst256 >> 4) == lax.rem(row, 8))
    lane4 = both(
        src256 == 16 * ((dst256 >> 2) & 15) + (dst256 & 3),
        ((dst256 >> 6) & 1) == lax.rem(row_in, 2),
    )
    tab_out[...] = onehot(
        jnp.logical_or(both(lane5, dst256 < LANES), both(lane4, dst256 >= LANES))
    )
    tab_64[...] = onehot(src128 == 64 * lax.rem(member, 2) + (dst128 & 63))
    tab_16[...] = onehot(src128 == 16 * lax.rem(col, 8) + (dst128 & 15))
    tab_h[...] = onehot(
        src128 == 64 * lax.rem(group, 2) + 16 * (dst128 >> 6) + (dst128 & 15)
    )
    tab_p4[...] = onehot(
        iota((TOK, 64), 0) == 16 * (iota((TOK, 64), 1) >> 2) + (iota((TOK, 64), 1) & 3)
    )
    tab_p5[...] = onehot(iota((TOK, 16), 0) == 16 * iota((TOK, 16), 1))

    def pair_forward(j, carry):
        lanes = pl.ds(pl.multiple_of(j * LANES, LANES), LANES)
        q, k, v, g = qp[:, lanes], kp[:, lanes], vp[:, lanes], gp[:, lanes]
        zero = jnp.zeros_like(k)
        i = j // 2
        for parity in range(2):
            mine = low256 if parity == 0 else jnp.logical_not(low256)
            scores = mm_nt(jnp.where(mine, k, zero), q)
            dprob = mm_nt(jnp.where(mine, v, zero), g)
            weights, stat = forward(scores, dprob)
            w_all[2 * j + parity] = weights
            d_all[2 * j + parity] = dprob
            st1[2 * lax.rem(j, 2) + parity, i] = stat
        return carry

    def packed_forward(query_side, key_side, unit):
        zero = jnp.zeros_like(key_side)
        scores = mm_nt(jnp.where(low256, key_side, zero), query_side)
        dprob = mm_nt(jnp.where(low256, zero, key_side), query_side)
        weights, stat = forward(scores, dprob)
        w_all[unit] = weights
        d_all[unit] = dprob
        return stat

    lax.fori_loop(0, PAIRS, pair_forward, 0)

    rows4 = pl.ds(pl.multiple_of(64 * row_in, 64), 64)
    rows5 = pl.ds(pl.multiple_of(16 * row, 16), 16)

    @pl.when(is3)
    def _():
        pick4 = onehot(
            iota((64, TOK), 1) == 16 * (iota((64, TOK), 0) >> 2) + (iota((64, TOK), 0) & 3)
        )
        pick5 = onehot(iota((16, TOK), 1) == 16 * iota((16, TOK), 0))
        arrive(recv3, 1)
        sel5[1] = mm(pick5, recv3[1]).astype(BF16)
        sel4[1] = mm(pick4, recv3[1]).astype(BF16)
        to_rows(lambda: sel5.at[1], recv5.at[1, rows5, :], 7, 16)
        to_rows(lambda: sel4.at[1], recv4.at[1, rows4, :], 6, 4)
        sel5[0] = mm(pick5, recv3[0]).astype(BF16)
        sel4[0] = mm(pick4, recv3[0]).astype(BF16)

    to_workers(lambda w, i: st1.at[w, i, :, lane_block(w >> 1)], a_own.at[col], 2)
    to_group(lambda w: st1.at[w, :, :, lane_block(w >> 1)], b_own.at[member], 3)

    arrive(recv_a, 0)
    for i in range(3):
        st2[i] = packed_forward(recv_a[i, 0], recv_a[i, 1], HEADS + i)
    for apart in range(3):
        i = lax.rem(group + apart, 3)
        copy = remote(
            st2.at[i], d_two.at[group], 5, row, member + 4 * i, sent_all if apart else sent_not3
        )
        if apart:
            copy.start()
        else:
            pl.when(is3)(lambda: local(st2.at[group], d_two.at[group], 5))
            pl.when(jnp.logical_not(is3))(copy.start)
    to_group(lambda w: st2.at[:, :, lane_block(w >> 1)], c_two.at[member], 4)

    kept4 = (lane & 15) < 4
    kept5 = (lane & 15) == 0

    def picked(moved, count, hit):
        total = jnp.zeros((8, TOK), F32)
        for step in range(count):
            total = total + jnp.where(hit(step), moved[step], 0.0)
        return total

    @pl.when(is3)
    def _():
        to_rows(lambda: sel5.at[0], recv5.at[0, rows5, :], 13, 16)
        to_rows(lambda: sel4.at[0], recv4.at[0, rows4, :], 12, 4)

    @pl.when(is3)
    def _():
        st_l[0] = packed_forward(recv3[0], recv3[1], 15)
        arrive(a_own, 2)
        arrive(d_two, 5)
        one = move(a_own[...].reshape(16 * 8, LANES), tab_a[...]).reshape(16, 8, TOK)
        one = rows_of(picked(one, 16, lambda c: (lane >> 4) == c))
        two = move(d_two[...].reshape(4 * 8, TOK), tab_d[...]).reshape(4, 8, TOK)
        two = rows_of(picked(two, 4, lambda c: (lane >> 6) == c))
        early = merge([one, two, rows_of(st_l[0])])
        arrive(recv4.at[1], 6)
        arrive(recv5.at[1], 7)
        st_l[1] = packed_forward(recv3[0], recv4[1], 16)
        st_l[2] = packed_forward(recv3[0], recv5[1], 17)
        lse, delta = merge(
            [early, masked_rows(st_l[1], kept4), masked_rows(st_l[2], kept5)]
        )
        final = stat_tile(lse, delta, 0.0)
        st3[...] = final

        def block(to_col):
            return st3.at[:, lane_block(to_col >> 3)]

        moved = move(final, tab_out[...])
        st5_out[...] = moved[0:2, :LANES]
        st4_out[...] = moved[0:2, LANES:]
        to_rows(lambda: st5_out, j_three.at[row], 11, 16)
        to_rows(lambda: st4_out, i_three.at[row_in], 10, 4)
        to_cols(
            [4 * ((group + apart) & 3) + member for apart in range(1, 4)],
            block, h_three.at[group], 9,
        )
        local(block(col), h_three.at[group], 9)
        to_cols(
            [
                4 * ((group + apart) & 3) + ((member + beside) & 3)
                for beside in range(1, 4)
                for apart in range(4)
            ],
            block, g_three.at[member, group], 8,
        )

    def packed_backward(query_side, key_side, unit, stat, final):
        probs, dscore = backward(
            w_all[unit], d_all[unit], stat[2:3], final[0:1], final[1:2]
        )
        zero = jnp.zeros_like(key_side)
        both = mm(dscore, jnp.where(low256, query_side, zero)) + mm(
            probs, jnp.where(low256, zero, query_side)
        )
        return both, mm_tn(dscore, jnp.where(low256, key_side, zero))

    others_of_row = [lax.rem(col + apart, 16) for apart in range(1, 16)]

    def rows_of_owner(slot, to_col):
        return out_l.at[slot, pl.ds(pl.multiple_of(16 * to_col, 16), 16), :]

    def low_part(tile, low):
        return jnp.where(low, tile, jnp.zeros_like(tile))

    def high_part(tile, low):
        return jnp.where(low, jnp.zeros_like(tile), tile)

    @pl.when(is3)
    def _():
        pair3, own = packed_backward(recv3[0], recv3[1], 15, st_l[0], st3[...])
        base3[...] = pair3
        for unit, keys_of, kept in ((1, recv4, kept4), (2, recv5, kept5)):
            _, dscore = backward(
                w_all[15 + unit], d_all[15 + unit],
                jnp.where(kept, st_l[unit, 2:3], NEG_FILL), st3[0:1], st3[1:2],
            )
            own = own + mm_tn(dscore, low_part(keys_of[1], low256))
        out_l[1] = own.astype(BF16)
        to_cols(others_of_row, lambda to_col: rows_of_owner(1, to_col), back3.at[col, 1], 16)
        local(rows_of_owner(1, col), back3.at[col, 1], 16)
        arrive(recv4.at[0], 12)
        arrive(recv5.at[0], 13)
        for keyed, own_rows, others in ((keyed4, sel4, recv4), (keyed5, sel5, recv5)):
            low = iota(own_rows.shape[1:], 1) < HEAD_DIM
            keyed[0] = mm_nt(low_part(own_rows[1], low), others[0])
            keyed[1] = mm_nt(high_part(own_rows[1], low), others[0])

    arrive(b_own, 3)
    arrive(h_three, 9)
    local(h_three, g_three.at[member], 8)
    own2 = move(b_own[...].reshape(4 * 3 * 8, LANES), tab_64[...]).reshape(4, 3, 8, TOK)
    long2 = move(h_three[...].reshape(3 * 8, LANES), tab_h[...]).reshape(3, 8, TOK)
    for i in range(3):
        one = rows_of(picked(own2[:, i], 4, lambda c: (lane >> 6) == c))
        lse, delta = merge([one, rows_of(st2[i])])
        long = ((lane >> 4) & 3) == i
        fin2[i] = stat_tile(
            jnp.where(long, long2[i][0:1], lse), jnp.where(long, long2[i][1:2], delta), 0.0
        )

    swapped = []
    for i in range(3):
        pair, own = packed_backward(recv_a[i, 0], recv_a[i, 1], HEADS + i, st2[i], fin2[i])
        out2[i] = pair.astype(BF16)
        swapped.append(own)
    out2[3] = (swapped[0] + swap(swapped[1])).astype(BF16)
    out2[4] = swapped[2].astype(BF16)
    to_group(
        lambda w: out2.at[3:5, pl.ds(pl.multiple_of(64 * w, 64), 64), :],
        back2.at[member, 3:5], 14,
    )

    @pl.when(is3)
    def _():
        def keyed_backward(keyed, total, others):
            probs = jnp.exp(keyed[0] - total[0:1])
            dscore = probs * (keyed[1] - total[1:2])
            pair = mm(dscore.astype(BF16), low_part(others[0], low256)) + mm(
                probs.astype(BF16), high_part(others[0], low256)
            )
            return pair.astype(BF16)

        arrive(i_three, 10)
        arrive(j_three, 11)
        total4 = jnp.concatenate([i_three[0] + i_three[1], i_three[2] + i_three[3]], axis=1)
        total5 = jnp.concatenate(
            [jnp.sum(j_three[0:8], axis=0), jnp.sum(j_three[8:16], axis=0)], axis=1
        )
        pair = (
            base3[...]
            + mm(tab_p4[...], keyed_backward(keyed4, total4, recv4))
            + mm(tab_p5[...], keyed_backward(keyed5, total5, recv5))
        )
        out_l[0] = pair.astype(BF16)

        to_cols(others_of_row, lambda to_col: rows_of_owner(0, to_col), back3.at[col, 0], 15)
        local(rows_of_owner(0, col), back3.at[col, 0], 15)

    to_group(
        lambda w: out2.at[0:3, pl.ds(pl.multiple_of(64 * w, 64), 64), :],
        back2.at[member, 0:3], 14,
    )

    arrive(c_two, 4)
    arrive(g_three, 8)
    two1 = move(c_two[...].reshape(HEADS * 8, LANES), tab_64[...]).reshape(4, 3, 8, TOK)
    three1 = move(g_three[...].reshape(HEADS * 8, LANES), tab_16[...]).reshape(4, 3, 8, TOK)
    for h in range(HEADS):
        w, i = h % 4, h // 4
        one = rows_of(st1[w, i])
        lse, delta = merge([one, masked_rows(two1[w, i], (lane >> 6) == w)])
        long = (lane >> 4) == 4 * w + i
        fin1[h] = stat_tile(
            jnp.where(long, three1[w, i][0:1], lse), jnp.where(long, three1[w, i][1:2], delta), 0.0
        )

    def pair_backward(j, carry):
        lanes = pl.ds(pl.multiple_of(j * LANES, LANES), LANES)
        q, k, g = qp[:, lanes], kp[:, lanes], gp[:, lanes]
        zero = jnp.zeros_like(k)
        i = j // 2
        sum_q = sum_k = sum_v = 0.0
        for parity in range(2):
            mine = low256 if parity == 0 else jnp.logical_not(low256)
            h = 2 * j + parity
            stat = st1[2 * lax.rem(j, 2) + parity, i]
            final = fin1[h]
            probs, dscore = backward(w_all[h], d_all[h], stat[2:3], final[0:1], final[1:2])
            sum_v = sum_v + mm(probs, jnp.where(mine, g, zero))
            sum_k = sum_k + mm(dscore, jnp.where(mine, q, zero))
            sum_q = sum_q + mm_tn(dscore, jnp.where(mine, k, zero))
        acc_q[:, lanes] = sum_q
        acc_k[:, lanes] = sum_k
        acc_v[:, lanes] = sum_v
        return carry

    lax.fori_loop(0, PAIRS, pair_backward, 0)

    for left in sent_all:
        left()

    @pl.when(is3)
    def _():
        for left in sent3:
            left()

    @pl.when(jnp.logical_not(is3))
    def _():
        for left in sent_not3:
            left()

    def returned(w, count, pair, own, own_low):
        low = iota((count, LANES), 1) < HEAD_DIM
        pair = pair.astype(F32)
        own = own.astype(F32)
        other = swap(pair)
        if (w % 2 == 0) != own_low:
            own = swap(own)
        if w % 2 == 0:
            return [jnp.where(low, part, 0.0) for part in (own, pair, other)]
        return [jnp.where(low, 0.0, part) for part in (own, other, pair)]

    heads = [
        (h, h % 4, h // 4, slice(LANES * (h // 2), LANES * (h // 2) + LANES))
        for h in range(HEADS)
    ]
    sums = ((acc_q, sum_q), (acc_k, sum_k), (acc_v, sum_v))
    arrive(back2, 14)
    for h, w, i, tile in heads:
        rows = slice(64 * w, 64 * w + 64)
        parts = returned(w, 64, back2[w, i], back2[w, 3 + i // 2], i != 1)
        for part, (acc, _) in zip(parts, sums):
            acc[rows, tile] += part
    for (acc, out), factor in zip(sums, (SCALE, 1.0, 1.0)):
        out[...] = (acc[...] * factor).astype(BF16)
    arrive(back3.at[:, 1], 16)
    arrive(back3.at[:, 0], 15)
    for h, w, i, tile in heads:
        rows = slice(64 * w + 16 * i, 64 * w + 16 * i + 16)
        parts = returned(w, 16, back3[h, 0], back3[h, 1], True)
        for part, (acc, out), factor in zip(parts, sums, (SCALE, 1.0, 1.0)):
            out[rows, tile] = ((acc[rows, tile] + part) * factor).astype(BF16)


def restore(sum_q, sum_k, sum_v, order, dq_hbm, dk_hbm, dv_hbm, dq, dk, dv, sems):
    copies = []
    for slot, (src, tile, dst) in enumerate(
        ((sum_q, dq, dq_hbm), (sum_k, dk, dk_hbm), (sum_v, dv, dv_hbm))
    ):
        tile[...] = mm(order[...], src[...]).astype(BF16)
        copy = pltpu.make_async_copy(tile, dst, sems.at[slot])
        copy.start()
        copies.append(copy)
    for copy in copies:
        copy.wait()


def body(queries, keys, values, grad_out):
    vm = pltpu.VMEM
    whole = pl.BlockSpec(memory_space=pltpu.VMEM)
    hbm = pl.BlockSpec(memory_space=pltpu.HBM)
    array = jax.ShapeDtypeStruct((TOK, WIDTH), BF16)
    queries, keys, values, grad_out = [
        pltpu.with_memory_space_constraint(x, pltpu.HBM) for x in (queries, keys, values, grad_out)
    ]
    sums = pl.pallas_call(
        kernel,
        out_shape=[array] * 3 + [jax.ShapeDtypeStruct((TOK, TOK), BF16)],
        in_specs=[hbm] * 4,
        out_specs=[whole] * 4,
        scratch_shapes=[vm((TOK, WIDTH), BF16)] * 8
        + [vm((TOK, WIDTH), F32)] * 3
        + [
            vm((18, TOK, TOK), F32),
            vm((18, TOK, TOK), F32),
            vm((4, 3, 2, 64, LANES), BF16),
            vm((3, 2, TOK, LANES), BF16),
            vm((2, TOK, LANES), BF16),
            vm((2, TOK, LANES), BF16),
            vm((2, TOK, LANES), BF16),
            vm((2, 64, LANES), BF16),
            vm((2, 16, LANES), BF16),
            vm((4, 3, 8, TOK), F32),
            vm((3, 8, TOK), F32),
            vm((3, 8, TOK), F32),
            vm((HEADS, 8, TOK), F32),
            vm((3, 8, TOK), F32),
            vm((8, TOK), F32),
            vm((2, LANES), F32),
            vm((2, LANES), F32),
            vm((16, 8, LANES), F32),
            vm((4, 3, 8, LANES), F32),
            vm((4, 3, 8, LANES), F32),
            vm((4, 8, TOK), F32),
            vm((4, 3, 8, LANES), F32),
            vm((3, 8, LANES), F32),
            vm((4, 2, LANES), F32),
            vm((16, 2, LANES), F32),
            vm((LANES, TOK), BF16),
            vm((TOK, TOK), BF16),
            vm((TOK, TOK), BF16),
            vm((LANES, TOK), BF16),
            vm((LANES, TOK), BF16),
            vm((LANES, TOK), BF16),
            vm((TOK, 64), BF16),
            vm((TOK, 16), BF16),
            vm((5, TOK, LANES), BF16),
            vm((2, TOK, LANES), BF16),
            vm((TOK, LANES), F32),
            vm((2, 64, TOK), F32),
            vm((2, 16, TOK), F32),
            vm((4, 5, 64, LANES), BF16),
            vm((HEADS, 2, 16, LANES), BF16),
            pltpu.SemaphoreType.DMA((160,)),
            pltpu.SemaphoreType.DMA((17,)),
            pltpu.SemaphoreType.DMA((4,)),
        ],
        compiler_params=pltpu.CompilerParams(
            collective_id=0, has_side_effects=True, vmem_limit_bytes=48 * 1024 * 1024
        ),
    )(queries, keys, values, grad_out)
    return pl.pallas_call(
        restore,
        out_shape=[array] * 3,
        in_specs=[whole] * 4,
        out_specs=[hbm] * 3,
        scratch_shapes=[vm((TOK, WIDTH), BF16)] * 3 + [pltpu.SemaphoreType.DMA((3,))],
        compiler_params=pltpu.CompilerParams(vmem_limit_bytes=16 * 1024 * 1024),
    )(*sums)


def solution(mesh):
    spec = P(("row", "col"), None)
    return jax.shard_map(
        body, mesh=mesh, in_specs=(spec,) * 4, out_specs=(spec,) * 3, check_vma=False
    )
```
